256 devices in a mesh: section: 2 (over z_hi), expert: 64 (over y, x, z_lo), tensor: 2 (over core).
Axes of the slice: x: 4, y: 4, z: 8 (z_hi: 2, z_lo: 4; z = z_hi * 4 + z_lo), core: 2. Of those that a mesh axis runs over, the one named last changes fastest.
Arguments:
- pre_kv: bfloat16 [4, 2, 2048, 8192], P(('section', 'tensor'), None, None, 'expert'), may hold values from -6 to 6
- pre_gate: float32 [4, 64, 2048], P(('section', 'tensor'), 'expert'), may hold values from -1 to 0, as said below
- pre_len: int32 [4], P(('section', 'tensor')), may hold values from 256 to 2048, as said below
- owners: int32 [4], P(('section', 'tensor')), may hold values from 0 to 7, as said below
- win_len: int32 [32], P(('section', 'tensor')), may hold values from 2 to 1024, as said below
- dec_qkv: bfloat16 [32, 3, 8192], P(('section', 'tensor'), None, 'expert'), may hold values from -256 to 256
- dec_gate: float32 [32, 64], P(('section', 'tensor'), 'expert'), may hold values from -1 to -0.05
- state_cache: bfloat16 [32, 64, 128, 128], P(('section', 'tensor'), 'expert'), may hold values from -12 to 12
- win_cache: bfloat16 [32, 2, 1024, 8192], P(('section', 'tensor'), None, None, 'expert'), may hold values from -7 to 7
- head_gain: float32 [2, 8192], P(None, 'expert'), may hold values from 0.1 to 1.9
- out_weight: bfloat16 [8192, 2048], P('expert'), may hold values from -0.1875 to 0.1875
- resid: bfloat16 [32, 2048], P(('section', 'tensor')), may hold values from -6 to 6
- moe_gain: float32 [2048], replicated, may hold values from 0.1 to 1.9
- router: bfloat16 [2048, 128], replicated, may hold values from -0.125 to 0.125
- routes: int32 [32, 8], replicated, may hold values from 0 to 127, all different within a row; in each aligned block of 32 rows (0 to 31, 32 to 63, ...) at most 4 rows name the same one
- w_in: bfloat16 [128, 2048, 2, 1024], P(('section', 'expert'), None, None, 'tensor'), may hold values from -0.125 to 0.125
- w_down: bfloat16 [128, 1024, 2048], P(('section', 'expert'), 'tensor'), may hold values from -0.75 to 0.75
Outputs:
- layer_out: bfloat16 [32, 2048], P(('section', 'tensor'), 'expert')
- new_state: float32 [32, 64, 128, 128], P(('section', 'tensor'), 'expert')
The draws below stay inside these ranges and needn't reach their ends.
Inputs may be any that keep to these rules, and one draw needn't show every extreme that they name: `pre_gate`: log decays; some heads forget within some tens of positions. `pre_len`: some request has length 2048. `owners`: a row within the block of 8 decode rows. `win_len`: the live positions are the last ones of the 1024; in the row that takes an incoming request it equals min(1024, that request's pre_len). `routes`: each row names 8 different experts; every expert is named by 1 to 4 of the 32 rows, a bound that some block reaches.
All inputs are finite; a program needn't handle non-finite values.
Results may differ from the reference program's by a relative error of at most 0.006.
Values may be sent and summed in bfloat16 or wider, within the bound.
No kernel may reach another device: no remote copies, remote signals or barrier semaphores. Data moves between devices by JAX's collectives and lax.ppermute only.
A program may use at most 64 MiB of HBM per device.

```python
import math
import jax
import jax.numpy as jnp
import numpy as np
from jax import lax

DH = 128
ATTENTION_HEADS = 64
HD = 8192
D = 2048
EF = 1024
EXPERTS = 128
TOPK = 8
WIN = 1024
PROMPT_LENGTH = 2048
ROWS_DEV = 8
PREFILL_REQUESTS = 4
ROWS = 32
CAP = 4


def shared_lengths(key):
    key_prompt, key_long, key_slots, key_full, key_live, key_wide = jax.random.split(key, 6)
    prompt = jax.random.randint(key_prompt, (PREFILL_REQUESTS,), PROMPT_LENGTH // 8, PROMPT_LENGTH + 1)
    longest = jax.random.randint(key_long, (), 0, PREFILL_REQUESTS)
    prompt = prompt.at[longest].set(PROMPT_LENGTH)
    slots = jax.random.randint(key_slots, (PREFILL_REQUESTS,), 0, ROWS_DEV)
    fullest = jax.random.randint(key_full, (), 0, PREFILL_REQUESTS)
    slots = slots.at[fullest].set(ROWS_DEV - 1)
    live = jax.random.randint(key_live, (ROWS,), 2, WIN + 1)
    blocks = jnp.arange(PREFILL_REQUESTS, dtype=jnp.int32)
    partner = (blocks + PREFILL_REQUESTS // 2) % PREFILL_REQUESTS
    live = live.at[blocks * ROWS_DEV + slots].set(jnp.minimum(prompt[partner], WIN))
    widest = jax.random.randint(key_wide, (), 0, PREFILL_REQUESTS)
    live = live.at[widest * ROWS_DEV + (slots[widest] + 1) % ROWS_DEV].set(WIN)
    return (prompt, slots, live)


def shared_keys(key):
    return jnp.clip(jax.random.normal(key, (ROWS, WIN, HD), jnp.float32), -6.0, 6.0)


def draw_pre_len(key, part):
    return shared_lengths(key)[0]


def draw_owners(key, part):
    return shared_lengths(key)[1]


def draw_win_len(key, part):
    return shared_lengths(key)[2]


def draw_pre_gate(key, part):
    key = jax.random.fold_in(key, 31)
    quick_rate_key, gradual_key, speedy_key, wobble_key, spike_key, drop_key = jax.random.split(key, 6)
    fast_share = 0.5
    fast = jax.random.uniform(quick_rate_key, (PREFILL_REQUESTS, ATTENTION_HEADS, 1)) < fast_share
    slow_rate = jnp.exp(jax.random.uniform(gradual_key, (PREFILL_REQUESTS, ATTENTION_HEADS, 1), minval=math.log(0.2 / PROMPT_LENGTH), maxval=math.log(1.5 / PROMPT_LENGTH)))
    fast_rate = jax.random.uniform(speedy_key, (PREFILL_REQUESTS, ATTENTION_HEADS, 1), minval=1.0 / 50.0, maxval=1.0 / 30.0)
    arrival_rate = jnp.where(fast, fast_rate, slow_rate)
    random_wobble = jnp.exp(jax.random.uniform(wobble_key, (PREFILL_REQUESTS, ATTENTION_HEADS, PROMPT_LENGTH), minval=math.log(0.5), maxval=math.log(2.0)))
    spike_sample = jax.random.uniform(spike_key, (PREFILL_REQUESTS, ATTENTION_HEADS, PROMPT_LENGTH))
    drop_fraction = jax.random.uniform(drop_key, (PREFILL_REQUESTS, ATTENTION_HEADS, PROMPT_LENGTH), minval=0.5, maxval=0.8)
    spike_amount = jnp.where(spike_sample < 3.0 / PROMPT_LENGTH, jnp.log(drop_fraction), 0.0)
    return (-arrival_rate * random_wobble + spike_amount).astype(jnp.float32)


def draw_win_cache(key, part):
    key_rows = shared_keys(key)
    key = jax.random.fold_in(key, 21)
    value_rows = jnp.clip(jax.random.normal(key, (ROWS, WIN, HD), jnp.float32), -6.0, 6.0)
    return jnp.stack([key_rows, value_rows], axis=1).astype(jnp.bfloat16)


def draw_dec_qkv(key, part):
    key = jax.random.fold_in(key, 22)
    tokens = jnp.clip(jax.random.normal(key, (ROWS, 3, HD), jnp.float32), -6.0, 6.0)
    return tokens.astype(jnp.bfloat16)


def strengthened(result, key, source, target, parts, factor):
    owner, partner = [(jnp.arange(result.shape[position]) // (result.shape[position] // parts)).reshape([-1 if axis == position else 1 for axis in range(result.ndim)]) for position in (source, target)]
    chosen = jax.random.permutation(key, parts)[partner]
    strong = (owner == chosen) | (owner == (partner + parts // 2) % parts)
    return jnp.where(strong, factor * result, result)


def shard_levels(key, shape, pieces, low, largest):
    loudness = 1.0
    for dim, shards_of in pieces:
        steps = jax.random.uniform(jax.random.fold_in(jax.random.fold_in(key, 6), dim), (shards_of,), jnp.float32, low / len(pieces), largest / len(pieces))
        loudness = loudness * jnp.repeat(jnp.exp(steps), shape[dim] // shards_of).reshape((-1,) + (1,) * (len(shape) - 1 - dim))
    return loudness


def assign_block(rng, own, number, rows, number_of, top, reach, skew):
    sequence = jax.random.permutation(rng, number_of)
    packed, common = load_shares(number_of, rows * top, reach, skew, True), load_shares(number_of, rows * top, reach, skew, False)
    places = jnp.arange(number_of)

    def named(sizes, offset_by):
        used = int((sizes > 0).sum())
        fixed = max(1, used // 4)
        shifted = fixed + (places - fixed + offset_by * (used - fixed)) % max(1, number_of - fixed)
        return jnp.zeros((number_of,), jnp.int32).at[sequence[jnp.where(places < fixed, places, shifted)]].set(jnp.asarray(sizes, jnp.int32))

    sizes = jnp.where(number % 4 == 0, named(packed, number // 4), named(common, number - number // 4 - 1))
    mixed = jax.random.permutation(jax.random.fold_in(own, 3), number_of)
    giver, taker = mixed[0:number_of // 2 * 2:2], mixed[1:number_of // 2 * 2:2]
    slack = jnp.minimum(sizes[giver] - 1, reach - sizes[taker]) // 2
    slack = jnp.where((giver == sequence[0]) | (taker == sequence[0]) | (sizes[taker] == 0), 0, jnp.maximum(slack, 0))
    shifted = jax.random.randint(jax.random.fold_in(own, 4), (number_of // 2,), 0, 1 << 20) % (slack + 1)
    sizes = sizes.at[giver].add(-shifted).at[taker].add(shifted)
    items = jnp.searchsorted(jnp.cumsum(sizes), jnp.arange(rows * top), side="right").astype(jnp.int32)
    listing = items.reshape(top, rows).T
    listing = listing[jax.random.permutation(jax.random.fold_in(own, 1), rows)]
    offset_by = jax.random.randint(jax.random.fold_in(own, 2), (rows, 1), 0, top)
    return jnp.take_along_axis(listing, (jnp.arange(top)[None, :] + offset_by) % top, axis=1)


def load_shares(number_of, total, most, skew, full):
    weights = [(1 << 20) // math.isqrt(standing ** skew) + 1 for standing in range(1, number_of + 1)]
    largest = most if full else min(most, max(-(-total // number_of), total * weights[0] // sum(weights)))
    least = 1 if total - largest >= number_of - 1 else 0
    given, spare = [largest] + [least] * (number_of - 1), total - largest - least * (number_of - 1)
    while spare > 0:
        movable = [i for i in range(1, number_of) if given[i] < largest] or [i for i in range(1, number_of) if given[i] < most]
        whole, left = sum([weights[i] for i in movable]), spare
        for i in movable:
            extra = min(most - given[i], max(1, left * weights[i] // whole), spare)
            given[i] = given[i] + extra
            spare = spare - extra
    return np.array(given)


def centred(rng, shape, deviation, reach, shards=(), kind=jnp.bfloat16):
    gain = shard_levels(rng, shape, shards, -0.22, 0.18) if shards else 1.0
    values = jax.random.normal(rng, shape, jnp.float32) * deviation * gain
    return jnp.minimum(jnp.maximum(values, -reach), reach).astype(kind)


def bell_draw_with(stream_key, extent, width, reach, shards, heavy, kind=jnp.bfloat16):
    drawn = width * jax.random.normal(stream_key, extent, jnp.float32)
    if shards:
        drawn = drawn * shard_levels(stream_key, extent, shards, -0.22, 0.18)
    return jnp.clip(strengthened(drawn, jax.random.fold_in(stream_key, 3), *heavy), -reach, reach).astype(kind)


def setup_inputs(seed: int = 0) -> dict:
    key_list = jax.random.split(jax.random.key(seed), 18)
    pre_kv = centred(key_list[0], (PREFILL_REQUESTS, 2, PROMPT_LENGTH, HD), 1.0, 6.0, ((0, 4), (3, 64)))
    pre_gate = draw_pre_gate(jax.random.fold_in(key_list[17], 71), 0)
    pre_len = draw_pre_len(jax.random.fold_in(key_list[17], 71), 0)
    owners = draw_owners(jax.random.fold_in(key_list[17], 71), 0)
    win_len = draw_win_len(jax.random.fold_in(key_list[17], 71), 0)
    dec_qkv = draw_dec_qkv(jax.random.fold_in(key_list[17], 71), 0)
    dec_gate = jnp.clip(-1.0 + 0.95 * jax.random.uniform(key_list[6], (ROWS, ATTENTION_HEADS), jnp.float32) ** shard_levels(key_list[6], (ROWS, ATTENTION_HEADS), ((0, 4), (1, 64)), -0.2, 0.2), -1.0, -0.05)
    state_cache = centred(key_list[7], (ROWS, ATTENTION_HEADS, DH, DH), 2.0, 12.0, ((0, 4), (1, 64)))
    win_cache = draw_win_cache(jax.random.fold_in(key_list[17], 71), 0)
    head_gain = jnp.clip(1.0 + 0.18 * jax.random.normal(key_list[9], (2, HD), jnp.float32), 0.1, 1.9)
    out_weight = bell_draw_with(key_list[10], (HD, D), HD ** -0.5, 0.1875, ((0, 64),), (0, 1, 64, 4.0))
    resid = centred(key_list[11], (ROWS, D), 1.0, 6.0, ((0, 4),))
    moe_gain = jnp.clip(1.0 + 0.18 * jax.random.normal(key_list[12], (D,), jnp.float32), 0.1, 1.9)
    router = centred(key_list[13], (D, EXPERTS), D ** -0.5, 0.125)
    routes_keys = jax.random.split(jax.random.fold_in(key_list[14], 1), ROWS // ROWS)
    routes_turns = jax.random.permutation(jax.random.fold_in(key_list[14], 3), ROWS // ROWS)
    routes = jax.vmap(lambda own, number: assign_block(jax.random.fold_in(key_list[14], 2), own, number, ROWS, EXPERTS, TOPK, CAP, 2))(routes_keys, routes_turns).reshape((ROWS, TOPK))
    w_in = centred(key_list[15], (EXPERTS, D, 2, EF), D ** -0.5, 0.125, ((0, 128), (3, 2)))
    w_down = bell_draw_with(key_list[16], (EXPERTS, EF, D), EF ** -0.5, 0.75, ((0, 128), (1, 2)), (0, 2, 128, 5.5))
    return dict(pre_kv=pre_kv, pre_gate=pre_gate, pre_len=pre_len, owners=owners, win_len=win_len, dec_qkv=dec_qkv, dec_gate=dec_gate, state_cache=state_cache, win_cache=win_cache, head_gain=head_gain, out_weight=out_weight, resid=resid, moe_gain=moe_gain, router=router, routes=routes, w_in=w_in, w_down=w_down)


def norm_rows(values, gain_row):
    return values * lax.rsqrt(lax.optimization_barrier(jnp.mean(values * values, axis=-1, keepdims=True)) + 1e-06) * gain_row

def prompt_pieces(inputs):
    prompt_kv, decays, length = inputs
    live_mask = jnp.arange(PROMPT_LENGTH) < length
    kept_decays = jnp.where(live_mask[None, :], decays, jnp.zeros_like(decays))
    suffix = lax.optimization_barrier(jnp.sum(kept_decays, axis=1, keepdims=True)) - jnp.cumsum(kept_decays, axis=1)
    token_weights = jnp.where(live_mask[None, :], jnp.exp(suffix), jnp.zeros_like(suffix))
    key_rows = prompt_kv[0].reshape(PROMPT_LENGTH, ATTENTION_HEADS, DH).astype(jnp.float32)
    scaled = (key_rows * token_weights.T[:, :, None]).astype(jnp.bfloat16)
    scaled = lax.optimization_barrier(scaled).astype(jnp.float32)
    value_rows = prompt_kv[1].reshape(PROMPT_LENGTH, ATTENTION_HEADS, DH).astype(jnp.float32)
    states = jnp.einsum('thd,the->hde', scaled, value_rows).astype(jnp.bfloat16)
    padded = jnp.concatenate([jnp.zeros((2, WIN, ATTENTION_HEADS * DH), prompt_kv.dtype), prompt_kv], axis=1)
    window = lax.dynamic_slice_in_dim(padded, length.astype(jnp.int32), WIN, 1)
    return (states, window)

def reference(pre_kv, pre_gate, pre_len, owners, win_len, dec_qkv, dec_gate, state_cache, win_cache, head_gain, out_weight, resid, moe_gain, router, routes, w_in, w_down):
    prompt_states, prompt_windows = lax.map(prompt_pieces, (pre_kv, pre_gate, pre_len))
    blocks = jnp.arange(PREFILL_REQUESTS, dtype=jnp.int32)
    partner = (blocks + PREFILL_REQUESTS // 2) % PREFILL_REQUESTS
    targets = (blocks * ROWS_DEV + owners).astype(jnp.int32)
    previous = state_cache.at[targets].set(prompt_states[partner])
    windows = win_cache.at[targets].set(prompt_windows[partner])
    gain_pair = head_gain.reshape(2, ATTENTION_HEADS, DH)
    score_scale = DH ** (-0.5)

    def decode_row(inputs):
        row_qkv, row_gate, prior, window_kv, live_len = inputs
        queries = row_qkv[0].reshape(ATTENTION_HEADS, DH).astype(jnp.float32)
        new_keys = row_qkv[1].reshape(ATTENTION_HEADS, DH).astype(jnp.float32)
        new_values = row_qkv[2].reshape(ATTENTION_HEADS, DH).astype(jnp.float32)
        states = jnp.exp(row_gate)[:, None, None] * prior.astype(jnp.float32) + new_keys[:, :, None] * new_values[:, None, :]
        linear_out = jnp.einsum('hd,hde->he', queries, states, precision=lax.Precision.HIGHEST)
        key_rows = window_kv[0].reshape(WIN, ATTENTION_HEADS, DH).astype(jnp.float32)
        value_rows = window_kv[1].reshape(WIN, ATTENTION_HEADS, DH).astype(jnp.float32)
        scores = jnp.einsum('hd,whd->hw', queries, key_rows) * score_scale
        self_score = lax.optimization_barrier(jnp.sum(queries * new_keys, axis=1)) * score_scale
        live_mask = jnp.arange(WIN) >= WIN - live_len
        row_peak = jnp.maximum(lax.optimization_barrier(jnp.max(jnp.where(live_mask[None, :], scores, -jnp.inf), axis=1)), self_score)
        probabilities = jnp.where(live_mask[None, :], jnp.exp(scores - row_peak[:, None]), jnp.zeros_like(scores)).astype(jnp.bfloat16)
        probabilities = lax.optimization_barrier(probabilities).astype(jnp.float32)
        self_prob = lax.optimization_barrier(jnp.exp(self_score - row_peak).astype(jnp.bfloat16)).astype(jnp.float32)
        numerator = jnp.einsum('hw,whd->hd', probabilities, value_rows) + self_prob[:, None] * new_values
        denominator = lax.optimization_barrier(jnp.sum(probabilities, axis=1)) + self_prob
        window_out = numerator / denominator[:, None]
        head_out = norm_rows(linear_out, gain_pair[0]) + norm_rows(window_out, gain_pair[1])
        return (head_out.astype(jnp.bfloat16).reshape(ATTENTION_HEADS * DH), states)
    head_rows, new_states = lax.map(decode_row, (dec_qkv, dec_gate, previous, windows, win_len))
    attended = jnp.dot(head_rows, out_weight, preferred_element_type=jnp.float32)
    hidden = (resid.astype(jnp.float32) + attended).astype(jnp.bfloat16)
    normed = norm_rows(hidden.astype(jnp.float32), moe_gain).astype(jnp.bfloat16)
    logits = jnp.dot(normed, router, preferred_element_type=jnp.float32)
    chosen = jax.nn.sigmoid(jnp.take_along_axis(logits, routes, axis=1))
    shares = chosen / lax.optimization_barrier(jnp.sum(chosen, axis=1, keepdims=True))
    gate_table = lax.optimization_barrier(jnp.sum(jnp.where(routes[:, :, None] == jnp.arange(EXPERTS, dtype=jnp.int32)[None, None, :], shares[:, :, None], jnp.zeros_like(shares)[:, :, None]), axis=1))

    def expert_step(running, inputs):
        weights_in, weights_down, column = inputs
        hidden_pre = jnp.dot(normed, weights_in.reshape(D, 2 * EF), preferred_element_type=jnp.float32)
        activated = (jax.nn.silu(hidden_pre[:, :EF]) * hidden_pre[:, EF:]).astype(jnp.bfloat16)
        return (running + column[:, None] * jnp.dot(activated, weights_down, preferred_element_type=jnp.float32), None)
    mixture = lax.scan(expert_step, jnp.zeros((ROWS, D), jnp.float32), (w_in, w_down, gate_table.T))[0]
    layer_out = (hidden.astype(jnp.float32) + mixture).astype(jnp.bfloat16)
    return (layer_out, new_states)
```

```python
import jax
import jax.numpy as jnp
from jax import lax
from jax.sharding import Mesh, PartitionSpec as P

GRID = ("y", "x", "z")
BLOCKS = ("s", "t")
F32 = jnp.float32
BF16 = jnp.bfloat16


def swap(shard, axis, flip):
    return lax.ppermute(shard, axis, [(i, i ^ flip) for i in range(lax.axis_size(axis))])


def norm_rows(values, gain_row):
    return values * lax.rsqrt(jnp.mean(values * values, axis=-1, keepdims=True) + 1e-06) * gain_row


def prompt_state(prompt_kv, decays, length):
    positions = jnp.arange(prompt_kv.shape[1])
    live = positions < length
    kept = jnp.where(live, decays, 0.0)
    suffix = jnp.sum(kept) - jnp.cumsum(kept)
    weights = jnp.where(live, jnp.exp(suffix), 0.0)
    scaled = (prompt_kv[0].astype(F32) * weights[:, None]).astype(BF16)
    return jnp.einsum("td,te->de", scaled, prompt_kv[1], preferred_element_type=F32).astype(BF16)


def window_part(queries, keys, values, live, self_score, scale):
    scores = jnp.einsum("rd,rwd->rw", queries, keys, preferred_element_type=F32) * scale
    peak = jnp.maximum(jnp.max(jnp.where(live, scores, -jnp.inf), axis=1), self_score)
    prob = jnp.where(live, jnp.exp(scores - peak[:, None]), 0.0).astype(BF16)
    prob = lax.optimization_barrier(prob)
    numerator = jnp.einsum("rw,rwd->rd", prob, values, preferred_element_type=F32)
    return peak, numerator, jnp.sum(prob.astype(F32), axis=1)


def on_device(
    pre_kv, pre_gate, pre_len, owners, win_len, dec_qkv, dec_gate, state_cache, win_cache,
    head_gain, out_weight, resid, moe_gain, router, routes, w_in, w_down,
):
    section, core = lax.axis_index("s"), lax.axis_index("t")
    row, col, deep = lax.axis_index("y"), lax.axis_index("x"), lax.axis_index("z")
    block = section * 2 + core
    lane_tile = row * 4 + col
    head = lane_tile * 4 + deep

    owner = owners[0]
    piece_all = lax.dynamic_slice(resid, (0, lane_tile * 128), (8, 128))
    mine = lax.dynamic_slice_in_dim(dec_qkv, owner, 1, 0)[0].astype(F32)
    message = jnp.concatenate(
        [
            mine,
            jnp.broadcast_to(lax.dynamic_slice_in_dim(dec_gate, owner, 1, 0), (1, 128)),
            lax.dynamic_slice_in_dim(piece_all, owner, 1, 0).astype(F32),
            jnp.full((3, 128), owner.astype(F32)),
        ],
        axis=0,
    )
    got = swap(message, "s", 1)
    flag = jnp.full((8, 128), owner.astype(F32))
    beside = swap(flag, "t", 1)
    across = swap(flag, BLOCKS, 3)

    prompt_kv = pre_kv[0]
    length = pre_len[0]
    fresh_state = prompt_state(prompt_kv, pre_gate[0, 0], length)
    got_state = swap(fresh_state, "s", 1)

    taken = jnp.arange(8) == owner
    guest = got[:3].astype(BF16)
    qkv = jnp.where(taken[:, None, None], guest[None], dec_qkv)
    gate = jnp.where(taken[:, None], got[3, 0], dec_gate)
    queries, keys, values = qkv[:, 0], qkv[:, 1], qkv[:, 2]
    scale = 128 ** (-0.5)
    self_raw = jnp.sum(queries.astype(F32) * keys.astype(F32), axis=1)
    self_score = self_raw * scale

    width = win_cache.shape[2]
    live = jnp.arange(width)[None, :] >= (width - win_len)[:, None]
    peak, numerator, denominator = window_part(
        queries, win_cache[:, 0], win_cache[:, 1], live, self_score, scale
    )
    places = jnp.arange(prompt_kv.shape[1])[None, :]
    inside = (places < length) & (places >= length - width)
    guest_self = jnp.sum(got[0] * got[1])[None] * scale
    guest_peak, guest_num, guest_den = window_part(
        guest[0][None], prompt_kv[0][None], prompt_kv[1][None], inside, guest_self, scale
    )
    peak = jnp.where(taken, guest_peak[0], peak)
    numerator = jnp.where(taken[:, None], guest_num, numerator)
    denominator = jnp.where(taken, guest_den[0], denominator)
    self_prob = lax.optimization_barrier(jnp.exp(self_score - peak).astype(BF16)).astype(F32)
    numerator = numerator + self_prob[:, None] * values.astype(F32)
    denominator = denominator + self_prob
    window_out = numerator / denominator[:, None]

    cached = state_cache[:, 0]
    used = jnp.where(taken[:, None, None], fresh_state[None], cached)
    linear_out = (
        jnp.exp(gate) * jnp.einsum("rd,rde->re", queries, used, preferred_element_type=F32)
        + self_raw[:, None] * values.astype(F32)
    )
    head_out = (norm_rows(linear_out, head_gain[0]) + norm_rows(window_out, head_gain[1])).astype(BF16)
    partial = jnp.dot(head_out, out_weight, preferred_element_type=F32)

    pieces = partial.reshape(4, 2, 16, 128).transpose(2, 0, 1, 3).reshape(64, 2, 128)
    attended = lax.all_to_all(pieces, GRID, 0, 0).sum(0)
    own_resid = jnp.where(taken[:, None], got[4], piece_all.astype(F32))
    own_resid = lax.dynamic_slice_in_dim(own_resid, deep * 2, 2, 0)
    hidden = (own_resid + attended).astype(BF16)
    every = lax.all_to_all(
        jnp.broadcast_to(hidden[None], (256, 2, 128)), ("s", "t", "y", "x", "z"), 0, 0
    )
    every = every.reshape(4, 16, 4, 2, 128).transpose(0, 2, 3, 1, 4).reshape(32, 2048)

    partner_owner = got[5, 0].astype(jnp.int32)
    beside_owner = beside[0, 0].astype(jnp.int32)
    across_owner = across[0, 0].astype(jnp.int32)
    ids = jnp.arange(32)
    their_block, their_row = ids // 8, ids % 8
    held = jnp.where(
        their_block == block, owner,
        jnp.where(their_block == (block ^ 2), partner_owner,
                  jnp.where(their_block == (block ^ 1), beside_owner, across_owner)),
    )
    held_partner = jnp.where(
        their_block == block, partner_owner,
        jnp.where(their_block == (block ^ 2), owner,
                  jnp.where(their_block == (block ^ 1), across_owner, beside_owner)),
    )
    source = jnp.where(their_row == held, (their_block ^ 2) * 8 + held_partner, ids)
    order = (source[:, None] == ids[None, :]).astype(BF16)
    every = jnp.dot(order, every, preferred_element_type=F32)

    normed = norm_rows(every, moe_gain).astype(BF16)
    logits = jnp.dot(normed, router, preferred_element_type=F32)
    expert_ids = jnp.arange(logits.shape[1], dtype=jnp.int32)
    named = routes[:, :, None] == expert_ids[None, None, :]
    picked = jnp.sum(jnp.where(named, logits[:, None, :], 0.0), axis=2)
    chosen = jax.nn.sigmoid(picked)
    shares = chosen / jnp.sum(chosen, axis=1, keepdims=True)
    expert_id = section * 64 + head
    own_gate = jnp.sum(jnp.where(routes == expert_id, shares, 0.0), axis=1)

    member = jnp.any(named, axis=1)
    below = (ids[:, None] > ids[None, :]).astype(F32)
    rank = jnp.dot(below, member.astype(F32))
    slot = jnp.where(member, rank, -1.0)
    own_slot = jnp.sum(jnp.where(expert_ids[None, :] == expert_id, slot, 0.0), axis=1)
    chooser = own_slot[None, :] == jnp.arange(4, dtype=F32)[:, None]
    rows_in = jnp.dot(chooser.astype(BF16), normed, preferred_element_type=F32).astype(BF16)
    gates = jnp.sum(jnp.where(chooser, own_gate[None, :], 0.0), axis=1)

    units = w_in.shape[3]
    pre = jnp.dot(rows_in, w_in[0].reshape(w_in.shape[1], 2 * units), preferred_element_type=F32)
    act = (jax.nn.silu(pre[:, :units]) * pre[:, units:]).astype(BF16)
    term = gates[:, None] * jnp.dot(act, w_down[0], preferred_element_type=F32)
    term = term.reshape(4, 16, 4, 32).transpose(2, 1, 0, 3).reshape(1, 64, 1, 128)
    term = jnp.broadcast_to(term, (4, 64, 1, 128)).reshape(256, 1, 128)
    back = lax.all_to_all(term, ("s", "t", "z", "y", "x"), 0, 0)
    back = back.reshape(2, 2, 4, 16, 4, 32)

    own_slots = lax.dynamic_slice_in_dim(slot, block * 8, 8, 0)
    own_slots = own_slots.reshape(8, 2, 16, 4).transpose(0, 1, 3, 2)
    use = (own_slots[:, :, None, :, :, None] == jnp.arange(4, dtype=F32)).astype(F32)
    use = jnp.broadcast_to(use, (8, 2, 2, 4, 16, 4))
    mixture = jnp.einsum(
        "rn,nc->rc", use.reshape(8, 1024), back.reshape(1024, 32), precision=lax.Precision.HIGHEST
    )
    own = lax.dynamic_slice(every, (block * 8, head * 32), (8, 32))
    layer_out = (own + mixture).astype(BF16)

    previous = jnp.where(taken[:, None, None], got_state[None], cached).astype(F32)
    own_k, own_v = dec_qkv[:, 1].astype(F32), dec_qkv[:, 2].astype(F32)
    states = jnp.exp(dec_gate)[:, :, None] * previous + own_k[:, :, None] * own_v[:, None, :]
    return layer_out, states[:, None]


def solution(mesh):
    fine = Mesh(mesh.devices.reshape(2, 4, 4, 4, 2), ("s", "y", "x", "z", "t"))
    placed = (
        P(BLOCKS, None, None, GRID),
        P(BLOCKS, GRID, None),
        P(BLOCKS),
        P(BLOCKS),
        P(BLOCKS),
        P(BLOCKS, None, GRID),
        P(BLOCKS, GRID),
        P(BLOCKS, GRID, None, None),
        P(BLOCKS, None, None, GRID),
        P(None, GRID),
        P(GRID, None),
        P(BLOCKS, None),
        P(),
        P(),
        P(),
        P(("s",) + GRID, None, None, "t"),
        P(("s",) + GRID, "t", None),
    )
    return jax.shard_map(
        on_device,
        mesh=fine,
        in_specs=placed,
        out_specs=(P(BLOCKS, GRID), P(BLOCKS, GRID, None, None)),
        check_vma=False,
    )
```

```python
import jax
import jax.numpy as jnp
from jax import lax
from jax.experimental import pallas as pl
from jax.experimental.pallas import tpu as pltpu
from jax.sharding import Mesh, PartitionSpec as P

GRID = ("y", "x", "z")
BLOCKS = ("s", "t")
F32 = jnp.float32
BF16 = jnp.bfloat16
EXACT = lax.Precision.HIGHEST
SCALE = 128 ** (-0.5)

ANY = pl.BlockSpec(memory_space=pl.ANY)
HBM = pl.BlockSpec(memory_space=pl.ANY)
VMEM = pl.BlockSpec(memory_space=pltpu.VMEM)
SMEM = pl.BlockSpec(memory_space=pltpu.SMEM)


def params(mib):
    return pltpu.CompilerParams(vmem_limit_bytes=int(mib * 1024 * 1024))


def stay(*arrays):
    return [pltpu.with_memory_space_constraint(a, pltpu.HBM) for a in arrays]


def swap(shard, axis, flip):
    return lax.ppermute(shard, axis, [(i, i ^ flip) for i in range(lax.axis_size(axis))])


def iota(shape, axis):
    return lax.broadcasted_iota(jnp.int32, shape, axis)


def norm_rows(values, gain_row):
    return values * lax.rsqrt(jnp.mean(values * values, axis=-1, keepdims=True) + 1e-06) * gain_row


def dot(a, b, precision=None):
    return jnp.dot(a, b, preferred_element_type=F32, precision=precision)


def dot_t(a, b):
    return lax.dot_general(a, b, (((1,), (1,)), ((), ())), preferred_element_type=F32)


def own_block():
    return lax.axis_index("s") * 2 + lax.axis_index("t")


def message_kernel(
    owner_ref, gate_hbm, qkv_hbm, resid_hbm, out_ref, gate_ref, qkv_ref, resid_ref, sems
):
    tile = lax.axis_index("y") * 4 + lax.axis_index("x")
    columns = pl.ds(pl.multiple_of(tile * 128, 128), 128)
    copies = [
        pltpu.make_async_copy(qkv_hbm, qkv_ref, sems.at[0]),
        pltpu.make_async_copy(resid_hbm.at[:, columns], resid_ref, sems.at[1]),
        pltpu.make_async_copy(gate_hbm, gate_ref, sems.at[2]),
    ]
    for copy in copies:
        copy.start()
    for copy in copies:
        copy.wait()
    owner = owner_ref[0]
    taken = iota((8, 128), 0) == owner
    out_ref[5:8, :] = jnp.full((3, 128), owner.astype(F32), F32)
    for part in range(3):
        rows = qkv_ref[part].astype(F32)
        out_ref[part : part + 1, :] = jnp.sum(jnp.where(taken, rows, 0.0), axis=0, keepdims=True)
    out_ref[3:4, :] = jnp.full((1, 128), gate_ref[owner], F32)
    piece = resid_ref[...].astype(F32)
    out_ref[4:5, :] = jnp.sum(jnp.where(taken, piece, 0.0), axis=0, keepdims=True)


def own_rows_kernel(
    length_ref, live_hbm, gate_hbm, decay_hbm, qkv_hbm, gain_hbm, kv_hbm, cache_hbm, state_hbm,
    head_ref, fresh_ref, live_ref, gate_ref, decay_ref, qkv_ref, gain_ref, kv_ref, cache_ref, state_ref,
    small_sem, kv_sem, cache_sem, state_sem,
):
    small = [
        (decay_hbm, decay_ref), (qkv_hbm, qkv_ref), (live_hbm, live_ref),
        (gate_hbm, gate_ref), (gain_hbm, gain_ref),
    ]
    small_copies = [pltpu.make_async_copy(a, b, small_sem.at[i]) for i, (a, b) in enumerate(small)]
    kv_copies = [pltpu.make_async_copy(kv_hbm.at[i], kv_ref.at[i], kv_sem.at[i]) for i in range(2)]
    state_copy = pltpu.make_async_copy(state_hbm, state_ref, state_sem)
    cache_copies = [
        pltpu.make_async_copy(cache_hbm.at[r], cache_ref.at[r], cache_sem.at[r]) for r in range(8)
    ]
    for copy in small_copies + kv_copies + cache_copies + [state_copy]:
        copy.start()

    for copy in small_copies:
        copy.wait()
    length = length_ref[0]
    places = iota((16, 128), 0) * 128 + iota((16, 128), 1)
    kept = jnp.where(places < length, decay_ref[...], 0.0)
    later = (iota((128, 128), 0) > iota((128, 128), 1)).astype(F32)
    later_rows = (iota((16, 16), 1) > iota((16, 16), 0)).astype(F32)
    totals = jnp.broadcast_to(jnp.sum(kept, axis=1, keepdims=True), (16, 128))
    suffix = dot(kept, later, EXACT) + dot(later_rows, totals, EXACT)
    weights = jnp.where(places < length, jnp.exp(suffix), 0.0)

    for copy in kv_copies:
        copy.wait()
    fresh = jnp.zeros((128, 128), F32)
    for i in range(16):
        rows = pl.ds(i * 128, 128)
        turned = kv_ref[0, rows, :].astype(F32).T
        scaled = (turned * weights[i : i + 1, :]).astype(BF16)
        fresh += dot(scaled, kv_ref[1, rows, :])
    fresh_ref[...] = fresh.astype(BF16)

    queries = qkv_ref[0]
    q32, k32, v32 = queries.astype(F32), qkv_ref[1].astype(F32), qkv_ref[2].astype(F32)
    self_raw = jnp.sum(q32 * k32, axis=1, keepdims=True)
    self_score = self_raw * SCALE
    scores = jnp.zeros((8, 1024), F32)
    live = jnp.zeros((8, 1024), jnp.int32)
    gate = jnp.zeros((8, 128), F32)
    for r in range(8):
        cache_copies[r].wait()
        scores = jnp.where(iota((8, 1024), 0) == r, dot_t(queries, cache_ref[r, 0]), scores)
        live = jnp.where(iota((8, 1024), 0) == r, live_ref[r], live)
        gate = jnp.where(iota((8, 128), 0) == r, gate_ref[r], gate)
    scores = scores * SCALE
    alive = iota((8, 1024), 1) >= 1024 - live
    peak = jnp.max(jnp.where(alive, scores, -jnp.inf), axis=1, keepdims=True)
    peak = jnp.maximum(peak, self_score)
    prob = jnp.where(alive, jnp.exp(scores - peak), 0.0).astype(BF16)
    self_prob = jnp.exp(self_score - peak).astype(BF16).astype(F32)
    below = jnp.sum(prob.astype(F32), axis=1, keepdims=True) + self_prob
    above = jnp.zeros((8, 128), F32)
    linear = jnp.zeros((8, 128), F32)
    state_copy.wait()
    for r in range(8):
        mine = iota((8, 128), 0) == r
        above = jnp.where(mine, dot(prob, cache_ref[r, 1]), above)
        linear = jnp.where(mine, dot(queries, state_ref[r]), linear)
    window_out = (above + self_prob * v32) / below
    linear_out = jnp.exp(gate) * linear + self_raw * v32
    head_ref[...] = norm_rows(linear_out, gain_ref[0:1, :]) + norm_rows(window_out, gain_ref[1:2, :])


def guest_kernel(
    owner_ref, length_ref, got_ref, head_ref, fresh_ref, gain_hbm, kv_hbm, weight_hbm,
    out_ref, pack_ref, gain_ref, kv_ref, weight_ref, small_sem, kv_sem, weight_sem,
):
    small_copies = [pltpu.make_async_copy(gain_hbm, gain_ref, small_sem)]
    kv_copies = [pltpu.make_async_copy(kv_hbm.at[i], kv_ref.at[i], kv_sem.at[i]) for i in range(2)]
    weight_copy = pltpu.make_async_copy(weight_hbm, weight_ref, weight_sem)
    for copy in small_copies + kv_copies + [weight_copy]:
        copy.start()
    for copy in small_copies:
        copy.wait()
    length = length_ref[0]
    mine = jnp.full((8, 128), owner_ref[0].astype(F32), F32)
    pack_ref[...] = jnp.where(iota((8, 128), 0) == 0, mine, got_ref[5:6, :])
    q32 = jnp.broadcast_to(got_ref[0:1, :], (8, 128))
    k32 = jnp.broadcast_to(got_ref[1:2, :], (8, 128))
    v32 = jnp.broadcast_to(got_ref[2:3, :], (8, 128))
    query = q32.astype(BF16)
    self_raw = jnp.sum(q32 * k32, axis=1, keepdims=True)
    self_score = self_raw * SCALE
    linear_out = jnp.exp(got_ref[3:4, :]) * dot(query, fresh_ref[...]) + self_raw * v32
    kv_copies[0].wait()
    scores = dot_t(query, kv_ref[0]) * SCALE
    places = iota((8, 2048), 1)
    alive = (places < length) & (places >= length - 1024)
    peak = jnp.max(jnp.where(alive, scores, -jnp.inf), axis=1, keepdims=True)
    peak = jnp.maximum(peak, self_score)
    prob = jnp.where(alive, jnp.exp(scores - peak), 0.0).astype(BF16)
    self_prob = jnp.exp(self_score - peak).astype(BF16).astype(F32)
    below = jnp.sum(prob.astype(F32), axis=1, keepdims=True) + self_prob
    kv_copies[1].wait()
    window_out = (dot(prob, kv_ref[1]) + self_prob * v32) / below
    head = norm_rows(linear_out, gain_ref[0:1, :]) + norm_rows(window_out, gain_ref[1:2, :])
    head = jnp.where(iota((8, 128), 0) == owner_ref[0], head, head_ref[...]).astype(BF16)
    weight_copy.wait()
    for c in range(16):
        out_ref[c] = dot(head, weight_ref[:, c * 128 : (c + 1) * 128])


def named_by(routes_ref):
    lanes = iota((32, 128), 1)
    member = jnp.zeros((32, 128), F32)
    for k in range(8):
        member = jnp.where(routes_ref[:, k : k + 1] == lanes, 1.0, member)
    return member


def own_expert():
    return lax.axis_index("s") * 64 + lax.axis_index("y") * 16 + lax.axis_index("x") * 4 + lax.axis_index("z")


def prepare_kernel(
    pack_ref, beside_ref, routes_ref, turned_ref, order_ref, chooser_ref, member_ref, spread_ref, use_ref
):
    block = own_block()
    owner, partner = pack_ref[0, 0], pack_ref[1, 0]
    beside, across = beside_ref[0, 0], beside_ref[1, 0]
    ids = iota((32, 32), 0)
    their_block, their_row = ids // 8, (ids % 8).astype(F32)

    def by_block(mine, other, side, cross):
        return jnp.where(
            their_block == block, mine,
            jnp.where(their_block == (block ^ 2), other, jnp.where(their_block == (block ^ 1), side, cross)),
        )

    held = by_block(owner, partner, beside, across)
    held_partner = by_block(partner, owner, across, beside)
    source = jnp.where(
        their_row == held, ((their_block ^ 2) * 8).astype(F32) + held_partner, ids.astype(F32)
    )
    order = (source == iota((32, 32), 1).astype(F32)).astype(F32)
    order_ref[...] = order

    expert = own_expert()
    names_own = jnp.max((turned_ref[...] == expert).astype(F32), axis=0, keepdims=True)
    names_own = jnp.broadcast_to(names_own, (8, 32))
    upper = (iota((32, 32), 0) < iota((32, 32), 1)).astype(F32)
    rank = dot(names_own, upper)
    slots = (iota((8, 32), 0) % 4).astype(F32)
    chooser_ref[...] = jnp.where(names_own > 0, (rank == slots).astype(F32), 0.0)

    member = named_by(routes_ref)
    member_ref[...] = member
    spread_ref[...] = (iota((128, 1024), 1) // 8 == iota((128, 1024), 0)).astype(BF16)

    lower = (iota((32, 32), 1) < iota((32, 32), 0)).astype(F32)
    slot = jnp.where(member > 0, dot(lower, member), -1.0)
    first = (iota((8, 32), 1) == iota((8, 32), 0) + block * 8).astype(F32)
    slot = dot(first, slot)
    src = iota((128, 256), 1)
    sender = src // 128 * 64 + src % 16 * 4 + src // 16 % 4
    slot = dot(slot, (sender == iota((128, 256), 0)).astype(F32))
    for k in range(4):
        use_ref[k * 8 : (k + 1) * 8, :] = (slot == float(k)).astype(F32)


NEAR = 1024
CHUNK = 1024


def fetch_kernel(after_ref, router_hbm, in_hbm, down_hbm, router_ref, in_ref, down_ref, sems):
    copies = [
        pltpu.make_async_copy(router_hbm, router_ref, sems.at[0]),
        pltpu.make_async_copy(in_hbm.at[pl.ds(0, NEAR)], in_ref, sems.at[1]),
        pltpu.make_async_copy(down_hbm, down_ref, sems.at[2]),
    ]
    for copy in copies:
        copy.start()
    for copy in copies:
        copy.wait()


def expert_kernel(
    order_ref, chooser_ref, member_ref, spread_ref, gain_ref, hidden_ref, router_ref, near_ref, down_ref, in_hbm,
    out_ref, own_ref, in_ref, turn_ref, in_sem,
):
    in_copies = [
        pltpu.make_async_copy(
            in_hbm.at[pl.ds(NEAR + i * CHUNK, CHUNK)], in_ref.at[pl.ds(i * CHUNK, CHUNK)], in_sem.at[i]
        )
        for i in range((16384 - NEAR) // CHUNK)
    ]
    for copy in in_copies:
        copy.start()
    block = own_block()
    expert = own_expert()
    order, chooser, member = order_ref[...], chooser_ref[...], member_ref[...]

    scales = []
    for b in range(4):
        total = jnp.zeros((8, 128), F32)
        for c in range(16):
            x = hidden_ref[b * 16 + c].astype(F32)
            total += x * x
        scales.append(lax.rsqrt(jnp.sum(total, axis=1, keepdims=True) * (1.0 / 2048) + 1e-06))
    tiles = []
    for c in range(16):
        gain = gain_ref[:, c * 128 : (c + 1) * 128]
        parts = [hidden_ref[b * 16 + c].astype(F32) * scales[b] * gain for b in range(4)]
        tiles.append(jnp.concatenate(parts, axis=0).astype(BF16))
    normed = jnp.concatenate(tiles, axis=1)

    choose_gathered = dot(chooser, order)
    rows_in = dot(choose_gathered.astype(BF16), normed)

    logits = dot(order, dot(normed, router_ref[...]), EXACT)
    lanes = iota((32, 128), 1)
    chosen = member / (1.0 + jnp.exp(-logits))
    chosen = jnp.where(member > 0, chosen, 0.0)
    share = jnp.sum(jnp.where(lanes == expert, chosen, 0.0), axis=1, keepdims=True)
    share = share / jnp.sum(chosen, axis=1, keepdims=True)
    gates = dot(chooser, jnp.broadcast_to(share, (32, 128)), EXACT)

    stacked = jnp.concatenate([rows_in[:, c * 128 : (c + 1) * 128] for c in range(16)], axis=0)
    repeated = dot(stacked.astype(BF16), spread_ref[...])
    kind = iota((8, 1024), 1) % 8 - iota((8, 1024), 0) // 4
    pre = jnp.zeros((32, 128), F32)
    for c in range(16):
        piece = repeated[c * 8 : (c + 1) * 8, :]
        left = jnp.concatenate([jnp.where(kind == 2 * p, piece, 0.0) for p in range(4)], axis=0)
        start = c * 1024 - NEAR
        if start >= 0 and start % CHUNK == 0:
            in_copies[start // CHUNK].wait()
        right = near_ref[c * 1024 : (c + 1) * 1024, :] if start < 0 else in_ref[start : start + 1024, :]
        pre += dot(left.astype(BF16), right)
    acts = []
    for p in range(4):
        both = pre[p * 8 : (p + 1) * 8, :]
        acts.append(both / (1.0 + jnp.exp(-both)) * pltpu.roll(both, 4, 0))
    act = jnp.concatenate(acts, axis=1).astype(BF16)
    for c in range(16):
        turn_ref[c] = dot(act, down_ref[:, c * 128 : (c + 1) * 128]) * gates

    lane_block = iota((16, 128), 1) // 32
    by_slot = [turn_ref[:, k, :] for k in range(4)]
    for q in range(4):
        piece = jnp.zeros((16, 128), F32)
        for k in range(4):
            shift = (k - q) * 32 % 128
            moved = by_slot[k] if shift == 0 else pltpu.roll(by_slot[k], shift, 1)
            piece = jnp.where(lane_block == k, moved, piece)
        for b in range(4):
            out_ref[b * 64 + q * 16 : b * 64 + (q + 1) * 16, :] = piece

    tile = lax.axis_index("y") * 4 + lax.axis_index("x")
    raw = jnp.concatenate([hidden_ref[b * 16 + tile].astype(F32) for b in range(4)], axis=0)
    first = (iota((8, 32), 1) == iota((8, 32), 0) + block * 8).astype(F32)
    mine = dot(dot(first, order).astype(BF16), raw.astype(BF16))
    deep = lax.axis_index("z")
    own = mine
    for q in range(1, 4):
        own = jnp.where(deep == q, pltpu.roll(mine, 128 - q * 32, 1), own)
    own_ref[...] = own


def finish_kernel(use_ref, back_ref, own_ref, out_ref):
    back = back_ref[...]
    high = back.astype(BF16)
    low = (back - high.astype(F32)).astype(BF16)
    use = use_ref[...].astype(BF16)
    total = dot(use, high) + dot(use, low)
    out = own_ref[:, 0:32]
    for k in range(4):
        out += total[k * 8 : (k + 1) * 8, k * 32 : (k + 1) * 32]
    out_ref[...] = out.astype(BF16)


def on_device(
    pre_kv, pre_gate, pre_len, owners, win_len, dec_qkv, dec_gate, state_cache, win_cache,
    head_gain, out_weight, resid, moe_gain, router, routes, w_in, w_down,
):
    lane_tile = lax.axis_index("y") * 4 + lax.axis_index("x")
    deep = lax.axis_index("z")
    qkv = dec_qkv.transpose(1, 0, 2)
    gates = dec_gate.reshape(8)

    message = pl.pallas_call(
        message_kernel,
        out_shape=jax.ShapeDtypeStruct((8, 128), F32),
        in_specs=[SMEM] + [HBM] * 3,
        out_specs=VMEM,
        scratch_shapes=[
            pltpu.SMEM((8,), F32),
            pltpu.VMEM((3, 8, 128), BF16),
            pltpu.VMEM((8, 128), BF16),
            pltpu.SemaphoreType.DMA((3,)),
        ],
        compiler_params=params(2),
        name="message",
    )(owners, *stay(gates, qkv, resid))
    got = swap(message, "s", 1)

    own_heads, fresh_state = pl.pallas_call(
        own_rows_kernel,
        out_shape=(jax.ShapeDtypeStruct((8, 128), F32), jax.ShapeDtypeStruct((128, 128), BF16)),
        in_specs=[SMEM] + [HBM] * 8,
        out_specs=(VMEM, VMEM),
        scratch_shapes=[
            pltpu.SMEM((8,), jnp.int32),
            pltpu.SMEM((8,), F32),
            pltpu.VMEM((16, 128), F32),
            pltpu.VMEM((3, 8, 128), BF16),
            pltpu.VMEM((2, 128), F32),
            pltpu.VMEM((2, 2048, 128), BF16),
            pltpu.VMEM((8, 2, 1024, 128), BF16),
            pltpu.VMEM((8, 128, 128), BF16),
            pltpu.SemaphoreType.DMA((5,)),
            pltpu.SemaphoreType.DMA((2,)),
            pltpu.SemaphoreType.DMA((8,)),
            pltpu.SemaphoreType.DMA,
        ],
        compiler_params=params(14),
        name="own_rows",
    )(
        pre_len,
        *stay(
            win_len, gates, pre_gate.reshape(16, 128), qkv, head_gain,
            pre_kv[0], win_cache, state_cache[:, 0],
        )
    )
    got_state = swap(fresh_state, "s", 1)

    partial, pack = pl.pallas_call(
        guest_kernel,
        out_shape=(jax.ShapeDtypeStruct((16, 8, 128), F32), jax.ShapeDtypeStruct((8, 128), F32)),
        in_specs=[SMEM] * 2 + [VMEM] * 3 + [HBM] * 3,
        out_specs=(VMEM, VMEM),
        scratch_shapes=[
            pltpu.VMEM((2, 128), F32),
            pltpu.VMEM((2, 2048, 128), BF16),
            pltpu.VMEM((128, 2048), BF16),
            pltpu.SemaphoreType.DMA,
            pltpu.SemaphoreType.DMA((2,)),
            pltpu.SemaphoreType.DMA,
        ],
        compiler_params=params(8),
        name="guest",
    )(owners, pre_len, got, own_heads, fresh_state, *stay(head_gain, pre_kv[0], out_weight))
    beside = swap(pack, "t", 1)

    expert_in = w_in[0].reshape(2048, 2, 4, 128).transpose(0, 2, 1, 3).reshape(16384, 128)
    router_near, in_near, down_near = pl.pallas_call(
        fetch_kernel,
        out_shape=(
            pltpu.VMEM((2048, 128), BF16),
            pltpu.VMEM((NEAR, 128), BF16),
            pltpu.VMEM((512, 2048), BF16),
        ),
        in_specs=[ANY] + [HBM] * 3,
        out_specs=(VMEM,) * 3,
        scratch_shapes=[pltpu.SemaphoreType.DMA((3,))],
        compiler_params=params(2),
        name="fetch",
    )(pack, *stay(router, expert_in, w_down[0]))

    attended = lax.all_to_all(partial.reshape(64, 2, 128), GRID, 0, 0, tiled=True).sum(0)
    taken = jnp.arange(8) == owners[0]
    own_resid = lax.dynamic_slice(resid, (0, lane_tile * 128), (8, 128)).astype(F32)
    own_resid = jnp.where(taken[:, None], got[4], own_resid)
    own_resid = lax.dynamic_slice_in_dim(own_resid, deep * 2, 2, 0)
    hidden = (own_resid + attended).astype(BF16)
    hidden, router_near, in_near, down_near, beside = lax.optimization_barrier(
        (hidden, router_near, in_near, down_near, beside)
    )
    every = lax.all_to_all(
        jnp.broadcast_to(hidden[None], (256, 2, 128)), ("s", "t", "y", "x", "z"), 0, 0, tiled=True
    )

    order, chooser, member, spread, use = pl.pallas_call(
        prepare_kernel,
        out_shape=(
            jax.ShapeDtypeStruct((32, 32), F32),
            jax.ShapeDtypeStruct((8, 32), F32),
            jax.ShapeDtypeStruct((32, 128), F32),
            jax.ShapeDtypeStruct((128, 1024), BF16),
            jax.ShapeDtypeStruct((32, 256), F32),
        ),
        in_specs=[VMEM] * 4,
        out_specs=(VMEM,) * 5,
        compiler_params=params(4),
        name="prepare",
    )(pack, beside, routes, routes.T)
    term, own = pl.pallas_call(
        expert_kernel,
        out_shape=(jax.ShapeDtypeStruct((256, 128), F32), jax.ShapeDtypeStruct((8, 128), F32)),
        in_specs=[VMEM] * 9 + [HBM],
        out_specs=(VMEM, VMEM),
        scratch_shapes=[
            pltpu.VMEM((16384 - NEAR, 128), BF16),
            pltpu.VMEM((16, 8, 128), F32),
            pltpu.SemaphoreType.DMA(((16384 - NEAR) // CHUNK,)),
        ],
        compiler_params=params(12),
        name="experts",
    )(
        order, chooser, member, spread, moe_gain.reshape(1, 2048), every.reshape(64, 8, 128),
        router_near, in_near, down_near, *stay(expert_in),
    )
    back = lax.all_to_all(term.reshape(256, 1, 128), ("s", "t", "z", "y", "x"), 0, 0, tiled=True)
    layer_out = pl.pallas_call(
        finish_kernel,
        out_shape=jax.ShapeDtypeStruct((8, 32), BF16),
        in_specs=[VMEM] * 3,
        out_specs=VMEM,
        compiler_params=params(2),
        name="finish",
    )(use, back.reshape(256, 128), own)

    previous = jnp.where(taken[:, None, None], got_state[None], state_cache[:, 0]).astype(F32)
    own_k, own_v = dec_qkv[:, 1].astype(F32), dec_qkv[:, 2].astype(F32)
    states = jnp.exp(dec_gate)[:, :, None] * previous + own_k[:, :, None] * own_v[:, None, :]
    return layer_out, states[:, None]


def solution(mesh):
    fine = Mesh(mesh.devices.reshape(2, 4, 4, 4, 2), ("s", "y", "x", "z", "t"))
    placed = (
        P(BLOCKS, None, None, GRID),
        P(BLOCKS, GRID, None),
        P(BLOCKS),
        P(BLOCKS),
        P(BLOCKS),
        P(BLOCKS, None, GRID),
        P(BLOCKS, GRID),
        P(BLOCKS, GRID, None, None),
        P(BLOCKS, None, None, GRID),
        P(None, GRID),
        P(GRID, None),
        P(BLOCKS, None),
        P(),
        P(),
        P(),
        P(("s",) + GRID, None, None, "t"),
        P(("s",) + GRID, "t", None),
    )
    return jax.shard_map(
        on_device,
        mesh=fine,
        in_specs=placed,
        out_specs=(P(BLOCKS, GRID), P(BLOCKS, GRID, None, None)),
        check_vma=False,
    )
```

```python
import jax
import jax.numpy as jnp
from jax import lax
from jax.experimental import pallas as pl
from jax.experimental.pallas import tpu as pltpu
from jax.sharding import Mesh, PartitionSpec as P

GRID = ("y", "x", "z")
BLOCKS = ("s", "t")
F32 = jnp.float32
BF16 = jnp.bfloat16
EXACT = lax.Precision.HIGHEST
SCALE = 128 ** (-0.5)

ANY = pl.BlockSpec(memory_space=pl.ANY)
HBM = pl.BlockSpec(memory_space=pl.ANY)
VMEM = pl.BlockSpec(memory_space=pltpu.VMEM)
SMEM = pl.BlockSpec(memory_space=pltpu.SMEM)


def params(mib):
    return pltpu.CompilerParams(vmem_limit_bytes=int(mib * 1024 * 1024))


def stay(*arrays):
    return [pltpu.with_memory_space_constraint(a, pltpu.HBM) for a in arrays]


def swap(shard, axis, flip):
    return lax.ppermute(shard, axis, [(i, i ^ flip) for i in range(lax.axis_size(axis))])


def iota(shape, axis):
    return lax.broadcasted_iota(jnp.int32, shape, axis)


def norm_rows(values, gain_row):
    return values * lax.rsqrt(jnp.mean(values * values, axis=-1, keepdims=True) + 1e-06) * gain_row


def dot(a, b, precision=None):
    return jnp.dot(a, b, preferred_element_type=F32, precision=precision)


def dot_t(a, b):
    return lax.dot_general(a, b, (((1,), (1,)), ((), ())), preferred_element_type=F32)


def beside(*parts):
    return jnp.concatenate(parts, axis=1)


def split_rows(queries):
    odd = iota((8, 128), 0) % 2 == 1
    return beside(jnp.where(odd, 0.0, queries), jnp.where(odd, queries, 0.0)).astype(BF16)


def own_block():
    return lax.axis_index("s") * 2 + lax.axis_index("t")


def picked(rows, index):
    return jnp.sum(jnp.where(iota(rows.shape, 0) == index, rows, 0.0), axis=0, keepdims=True)


def message_kernel(owner_hbm, gate_hbm, qkv_hbm, resid_hbm, out_ref, owner_ref, gate_ref, qkv_ref, resid_ref, sems):
    pairs = [(owner_hbm, owner_ref), (gate_hbm, gate_ref), (qkv_hbm, qkv_ref), (resid_hbm, resid_ref)]
    copies = [pltpu.make_async_copy(a, b, sems.at[i]) for i, (a, b) in enumerate(pairs)]
    for copy in copies:
        copy.start()
    for copy in copies:
        copy.wait()
    owner = owner_ref[...]
    for part in range(3):
        out_ref[part : part + 1, :] = picked(qkv_ref[part].astype(F32), owner)
    gate = jnp.sum(jnp.where(iota((1, 8), 1) == owner, gate_ref[...], 0.0), axis=1, keepdims=True)
    out_ref[3:4, :] = jnp.broadcast_to(gate, (1, 128))
    out_ref[4:8, :] = jnp.broadcast_to(owner.astype(F32), (4, 128))
    row = picked(resid_ref[...].astype(F32), owner)
    for c in range(16):
        out_ref[8 + c : 9 + c, :] = row[:, c * 128 : (c + 1) * 128]


def own_rows_kernel(
    length_ref, live_hbm, gate_hbm, decay_hbm, qkv_hbm, gain_hbm, kv_hbm, cache_hbm, state_hbm,
    head_ref, fresh_ref, live_ref, gate_ref, decay_ref, qkv_ref, gain_ref, kv_ref, cache_ref, state_ref,
    small_sem, kv_sem, cache_sem, state_sem,
):
    small = [
        (decay_hbm, decay_ref), (qkv_hbm, qkv_ref), (live_hbm, live_ref),
        (gate_hbm, gate_ref), (gain_hbm, gain_ref),
    ]
    small_copies = [pltpu.make_async_copy(a, b, small_sem.at[i]) for i, (a, b) in enumerate(small)]
    kv_copies = [pltpu.make_async_copy(kv_hbm, kv_ref, kv_sem.at[0])]
    state_copy = pltpu.make_async_copy(state_hbm, state_ref, state_sem)
    cache_copies = [
        pltpu.make_async_copy(cache_hbm.at[pl.ds(2 * p, 2)], cache_ref.at[pl.ds(2 * p, 2)], cache_sem.at[p]) for p in range(4)
    ]
    for copy in small_copies + kv_copies + cache_copies + [state_copy]:
        copy.start()

    for copy in small_copies:
        copy.wait()
    length = length_ref[0]
    places = iota((16, 128), 0) * 128 + iota((16, 128), 1)
    kept = jnp.where(places < length, decay_ref[...], 0.0)
    later = (iota((128, 128), 0) > iota((128, 128), 1)).astype(F32)
    later_rows = (iota((16, 16), 1) > iota((16, 16), 0)).astype(F32)
    totals = jnp.broadcast_to(jnp.sum(kept, axis=1, keepdims=True), (16, 128))
    suffix = dot(kept, later, EXACT) + dot(later_rows, totals, EXACT)
    weights = jnp.where(places < length, jnp.exp(suffix), 0.0)

    for copy in kv_copies:
        copy.wait()
    fresh = jnp.zeros((128, 128), F32)
    for i in range(8):
        parts = []
        for j in (2 * i, 2 * i + 1):
            turned = kv_ref[0, j * 128 : (j + 1) * 128, :].T.astype(F32)
            parts.append((turned * weights[j : j + 1, :]).astype(BF16))
        fresh += dot(beside(*parts), kv_ref[1, i * 256 : (i + 1) * 256, :])
    fresh_ref[...] = fresh.astype(BF16)

    queries = qkv_ref[0]
    q32, k32, v32 = queries.astype(F32), qkv_ref[1].astype(F32), qkv_ref[2].astype(F32)
    self_raw = jnp.sum(q32 * k32, axis=1, keepdims=True)
    self_score = self_raw * SCALE
    scores = jnp.zeros((8, 1024), F32)
    live = jnp.zeros((8, 1024), jnp.int32)
    gate = jnp.zeros((8, 128), F32)
    halves = split_rows(q32)
    for r in range(8):
        live = jnp.where(iota((8, 1024), 0) == r, live_ref[r], live)
        gate = jnp.where(iota((8, 128), 0) == r, gate_ref[r], gate)
    for p in range(4):
        cache_copies[p].wait()
        both = dot_t(halves, beside(cache_ref[2 * p, 0], cache_ref[2 * p + 1, 0]))
        scores = jnp.where(iota((8, 1024), 0) // 2 == p, both, scores)
    scores = scores * SCALE
    alive = iota((8, 1024), 1) >= 1024 - live
    peak = jnp.max(jnp.where(alive, scores, -jnp.inf), axis=1, keepdims=True)
    peak = jnp.maximum(peak, self_score)
    prob = jnp.where(alive, jnp.exp(scores - peak), 0.0).astype(BF16)
    self_prob = jnp.exp(self_score - peak).astype(BF16).astype(F32)
    below = jnp.sum(prob.astype(F32), axis=1, keepdims=True) + self_prob
    above = jnp.zeros((8, 128), F32)
    linear = jnp.zeros((8, 128), F32)
    state_copy.wait()
    row = iota((8, 128), 0)
    for p in range(4):
        both = dot(prob, beside(cache_ref[2 * p, 1], cache_ref[2 * p + 1, 1]))
        above = jnp.where(row == 2 * p, both[:, :128], jnp.where(row == 2 * p + 1, both[:, 128:], above))
    for p in range(2):
        a, b, c, d = (state_ref[4 * p + i] for i in range(4))
        both = dot(halves, jnp.concatenate([beside(a, c), beside(b, d)], axis=0))
        linear = jnp.where(row // 2 == 2 * p, both[:, :128], jnp.where(row // 2 == 2 * p + 1, both[:, 128:], linear))
    window_out = (above + self_prob * v32) / below
    linear_out = jnp.exp(gate) * linear + self_raw * v32
    head_ref[...] = norm_rows(linear_out, gain_ref[0:1, :]) + norm_rows(window_out, gain_ref[1:2, :])


def guest_kernel(
    length_ref, message_ref, got_ref, head_ref, fresh_ref, gain_hbm, kv_ref, weight_ref,
    out_ref, pack_ref, gain_ref, gain_sem,
):
    gain_copy = pltpu.make_async_copy(gain_hbm, gain_ref, gain_sem)
    gain_copy.start()
    owner = message_ref[4:5, :]
    rows = iota((8, 128), 0).astype(F32)
    pack_ref[...] = jnp.where(rows == 0.0, owner, got_ref[4:5, :])
    q32, k32, v32 = got_ref[0:1, :], got_ref[1:2, :], got_ref[2:3, :]
    self_raw = jnp.sum(q32 * k32, axis=1, keepdims=True)
    self_score = self_raw * SCALE
    query = jnp.broadcast_to(q32, (8, 128))
    linear_out = jnp.exp(got_ref[3:4, :]) * dot(query.astype(BF16), fresh_ref[...])[0:1, :] + self_raw * v32

    scores = dot_t(split_rows(query), beside(kv_ref[0, 0:1024, :], kv_ref[0, 1024:2048, :])) * SCALE
    places = iota((8, 1024), 1) + iota((8, 1024), 0) % 2 * 1024
    length = length_ref[0]
    alive = (places < length) & (places >= length - 1024)
    peak = jnp.max(jnp.where(alive, scores, -jnp.inf), axis=1, keepdims=True)
    peak = jnp.maximum(jnp.maximum(peak[0:1, :], peak[1:2, :]), self_score)
    prob = jnp.where(alive, jnp.exp(scores - peak), 0.0).astype(BF16)
    self_prob = jnp.exp(self_score - peak).astype(BF16).astype(F32)
    total = jnp.sum(prob.astype(F32), axis=1, keepdims=True)
    below = total[0:1, :] + total[1:2, :] + self_prob
    both = dot(prob, beside(kv_ref[1, 0:1024, :], kv_ref[1, 1024:2048, :]))
    window_out = (both[0:1, :128] + both[1:2, 128:] + self_prob * v32) / below
    gain_copy.wait()
    head = norm_rows(linear_out, gain_ref[0:1, :]) + norm_rows(window_out, gain_ref[1:2, :])
    head = jnp.where(rows == owner, head, head_ref[...]).astype(BF16)
    for c in range(8):
        part = dot(head, weight_ref[:, c * 256 : (c + 1) * 256])
        out_ref[2 * c] = part[:, :128]
        out_ref[2 * c + 1] = part[:, 128:]


def named_by(turned_ref):
    turned = turned_ref[...]
    experts = iota((128, 32), 0)
    member = jnp.zeros((128, 32), F32)
    for k in range(8):
        member = jnp.where(turned[k : k + 1, :] == experts, 1.0, member)
    same = (iota((32, 32), 0) == iota((32, 32), 1)).astype(F32)
    return dot_t(same, member)


def own_expert():
    return lax.axis_index("s") * 64 + lax.axis_index("y") * 16 + lax.axis_index("x") * 4 + lax.axis_index("z")


def prepare_kernel(
    pack_ref, beside_ref, turned_ref, order_ref, chooser_ref, member_ref, spread_ref, use_ref
):
    block = own_block()
    owners = [pack_ref[0, 0], pack_ref[1, 0], beside_ref[0, 0], beside_ref[1, 0]]
    blocks = [block, block ^ 2, block ^ 1, block ^ 3]
    ids = iota((32, 32), 1)
    place, row = ids // 8, (ids % 8).astype(F32)
    target = jnp.zeros((32, 32), F32)
    for j in range(4):
        own = (blocks[j] * 8).astype(F32) + row
        other = (blocks[j ^ 1] * 8).astype(F32) + owners[j ^ 1]
        target = jnp.where(place == j, jnp.where(row == owners[j], other, own), target)
    order = (target == iota((32, 32), 0).astype(F32)).astype(F32)
    order_ref[...] = order

    expert = own_expert()
    names_own = jnp.max((turned_ref[...] == expert).astype(F32), axis=0, keepdims=True)
    names_own = jnp.broadcast_to(names_own, (8, 32))
    upper = (iota((32, 32), 0) < iota((32, 32), 1)).astype(F32)
    rank = dot(names_own, upper)
    slots = (iota((8, 32), 0) % 4).astype(F32)
    chooser_ref[...] = jnp.where(names_own > 0, (rank == slots).astype(F32), 0.0)

    member = named_by(turned_ref)
    member_ref[...] = member
    spread_ref[...] = (iota((128, 1024), 1) // 8 == iota((128, 1024), 0)).astype(BF16)

    lower = (iota((32, 32), 1) < iota((32, 32), 0)).astype(F32)
    slot = jnp.where(member > 0, dot(lower, member), -1.0)
    first = (iota((8, 32), 1) == iota((8, 32), 0) + block * 8).astype(F32)
    slot = dot(first, slot)
    src = iota((128, 256), 1)
    sender = src // 128 * 64 + src % 16 * 4 + src // 16 % 4
    slot = dot(slot, (sender == iota((128, 256), 0)).astype(F32))
    for k in range(4):
        use_ref[k * 8 : (k + 1) * 8, :] = (slot == float(k)).astype(F32)


def fetch_kernel(after_ref, router_hbm, in_hbm, router_ref, near_ref, sems):
    copies = [
        pltpu.make_async_copy(router_hbm, router_ref, sems.at[0]),
        pltpu.make_async_copy(in_hbm.at[pl.ds(0, 4096)], near_ref.at[pl.ds(0, 4096)], sems.at[1]),
        pltpu.make_async_copy(in_hbm.at[pl.ds(8192, 4096)], near_ref.at[pl.ds(4096, 4096)], sems.at[2]),
    ]
    for copy in copies:
        copy.start()
    for copy in copies:
        copy.wait()


def hidden_kernel(total_ref, message_ref, got_ref, resid_ref, fresh_ref, out_ref):
    taken = iota((8, 128), 0).astype(F32) == message_ref[4:5, :]
    for pair in range(8):
        parts = []
        for c in (2 * pair, 2 * pair + 1):
            rows = resid_ref[:, c * 128 : (c + 1) * 128].astype(F32)
            parts.append(jnp.where(taken, got_ref[8 + c : 9 + c, :], rows) + total_ref[c])
        out_ref[pair * 16 : (pair + 1) * 16, :] = jnp.concatenate(parts, axis=0).astype(BF16)
    out_ref[128:256, :] = fresh_ref[...]


def expert_kernel(
    order_ref, chooser_ref, member_ref, spread_ref, gain_ref, packet_ref, theirs_ref, next_ref, cross_ref, router_ref,
    near_ref, in_hbm, down_hbm,
    out_ref, own_ref, turn_ref, far_ref, down_ref, far_sem, down_sem,
):
    far_copies = []
    for half in range(2):
        for i in range(2):
            source = in_hbm.at[pl.ds(half * 8192 + 4096 + i * 2048, 2048)]
            target = far_ref.at[pl.ds(half * 4096 + i * 2048, 2048)]
            far_copies.append(pltpu.make_async_copy(source, target, far_sem.at[half * 2 + i]))
    down_copies = [
        pltpu.make_async_copy(down_hbm.at[pl.ds(i * 128, 128)], down_ref.at[pl.ds(i * 128, 128)], down_sem.at[i])
        for i in range(4)
    ]
    for i in (0, 2, 1, 3):
        far_copies[i].start()
    for copy in down_copies:
        copy.start()
    block = own_block()
    expert = own_expert()
    order, chooser, member = order_ref[...], chooser_ref[...], member_ref[...]

    hidden = []
    for ref in (packet_ref, theirs_ref, next_ref, cross_ref):
        two = [ref[pair * 16 : (pair + 1) * 16, :].astype(F32) for pair in range(8)]
        hidden.append([half for both in two for half in (both[:8, :], both[8:, :])])
    scales = []
    for rows in hidden:
        total = jnp.zeros((8, 128), F32)
        for x in rows:
            total += x * x
        scales.append(lax.rsqrt(jnp.sum(total, axis=1, keepdims=True) * (1.0 / 2048) + 1e-06))
    tiles = []
    for c in range(16):
        gain = gain_ref[:, c * 128 : (c + 1) * 128]
        parts = [hidden[j][c] * scales[j] * gain for j in range(4)]
        tiles.append(jnp.concatenate(parts, axis=0).astype(BF16))
    normed = jnp.concatenate(tiles, axis=1)

    choose_gathered = dot(chooser, order)
    rows_in = dot(choose_gathered.astype(BF16), normed)

    logits = dot(order, dot(normed, router_ref[...]), EXACT)
    lanes = iota((32, 128), 1)
    chosen = member / (1.0 + jnp.exp(-logits))
    chosen = jnp.where(member > 0, chosen, 0.0)
    share = jnp.sum(jnp.where(lanes == expert, chosen, 0.0), axis=1, keepdims=True)
    share = share / jnp.sum(chosen, axis=1, keepdims=True)
    gates = dot(chooser, jnp.broadcast_to(share, (32, 128)), EXACT)

    stacked = jnp.concatenate([rows_in[:, c * 128 : (c + 1) * 128] for c in range(16)], axis=0)
    repeated = dot(stacked.astype(BF16), spread_ref[...])
    kind = iota((8, 1024), 1) % 8 - iota((8, 1024), 0) // 4
    pre = jnp.zeros((64, 256), F32)
    for c in range(8):
        halves = [repeated[i * 8 : (i + 1) * 8, :] for i in (c, c + 8)]
        left = jnp.concatenate([jnp.where(kind == 2 * p, half, 0.0) for half in halves for p in range(4)], axis=0)
        if c >= 4 and c % 2 == 0:
            far_copies[c // 2 - 2].wait()
            far_copies[c // 2].wait()
        source, start = (near_ref, c * 1024) if c < 4 else (far_ref, (c - 4) * 1024)
        right = beside(source[start : start + 1024, :], source[start + 4096 : start + 5120, :])
        pre += dot(left.astype(BF16), right)
    pre = pre[:32, :128] + pre[32:, 128:]
    acts = []
    for p in range(4):
        both = pre[p * 8 : (p + 1) * 8, :]
        acts.append(both / (1.0 + jnp.exp(-both)) * pltpu.roll(both, 4, 0))
    act = jnp.concatenate(acts, axis=1).astype(BF16)
    for copy in down_copies:
        copy.wait()
    for c in range(8):
        part = dot(act, down_ref[:, c * 256 : (c + 1) * 256])
        turn_ref[2 * c] = part[:, :128] * gates
        turn_ref[2 * c + 1] = part[:, 128:] * gates

    lane_block = iota((16, 128), 1) // 32
    by_slot = [turn_ref[:, k, :] for k in range(4)]
    for q in range(4):
        piece = jnp.zeros((16, 128), F32)
        for k in range(4):
            shift = (k - q) * 32 % 128
            moved = by_slot[k] if shift == 0 else pltpu.roll(by_slot[k], shift, 1)
            piece = jnp.where(lane_block == k, moved, piece)
        for b in range(4):
            out_ref[b * 64 + q * 16 : b * 64 + (q + 1) * 16, :] = piece

    tile = lax.axis_index("y") * 4 + lax.axis_index("x")
    rows = pl.ds(pl.multiple_of(tile // 2 * 16, 16), 16)
    raw = []
    for ref in (packet_ref, theirs_ref, next_ref, cross_ref):
        both = ref[rows, :].astype(F32)
        raw.append(jnp.where(tile % 2 == 0, both[:8, :], both[8:, :]))
    raw = jnp.concatenate(raw, axis=0)
    first = (iota((8, 32), 1) == iota((8, 32), 0) + block * 8).astype(F32)
    mine = dot(dot(first, order).astype(BF16), raw.astype(BF16))
    deep = lax.axis_index("z")
    own = mine
    for q in range(1, 4):
        own = jnp.where(deep == q, pltpu.roll(mine, 128 - q * 32, 1), own)
    own_ref[...] = own


def finish_kernel(use_ref, back_ref, own_ref, out_ref):
    back = back_ref[...]
    high = back.astype(BF16)
    low = (back - high.astype(F32)).astype(BF16)
    use = use_ref[...].astype(BF16)
    total = dot(use, high) + dot(use, low)
    out = own_ref[:, 0:32]
    for k in range(4):
        out += total[k * 8 : (k + 1) * 8, k * 32 : (k + 1) * 32]
    out_ref[...] = out.astype(BF16)


def on_device(
    pre_kv, pre_gate, pre_len, owners, win_len, dec_qkv, dec_gate, state_cache, win_cache,
    head_gain, out_weight, resid, moe_gain, router, routes, w_in, w_down,
):
    qkv = dec_qkv.transpose(1, 0, 2)
    gates = dec_gate.reshape(8)

    message = pl.pallas_call(
        message_kernel,
        out_shape=jax.ShapeDtypeStruct((24, 128), F32),
        in_specs=[ANY] + [HBM] * 3,
        out_specs=VMEM,
        scratch_shapes=[
            pltpu.VMEM((1, 1), jnp.int32),
            pltpu.VMEM((1, 8), F32),
            pltpu.VMEM((3, 8, 128), BF16),
            pltpu.VMEM((8, 2048), BF16),
            pltpu.SemaphoreType.DMA((4,)),
        ],
        compiler_params=params(2),
        name="message",
    )(owners.reshape(1, 1), *stay(gates.reshape(1, 8), qkv, resid))
    got = swap(message, "s", 1)

    own_heads, fresh_state = pl.pallas_call(
        own_rows_kernel,
        out_shape=(jax.ShapeDtypeStruct((8, 128), F32), jax.ShapeDtypeStruct((128, 128), BF16)),
        in_specs=[SMEM] + [HBM] * 8,
        out_specs=(VMEM, VMEM),
        scratch_shapes=[
            pltpu.SMEM((8,), jnp.int32),
            pltpu.SMEM((8,), F32),
            pltpu.VMEM((16, 128), F32),
            pltpu.VMEM((3, 8, 128), BF16),
            pltpu.VMEM((2, 128), F32),
            pltpu.VMEM((2, 2048, 128), BF16),
            pltpu.VMEM((8, 2, 1024, 128), BF16),
            pltpu.VMEM((8, 128, 128), BF16),
            pltpu.SemaphoreType.DMA((5,)),
            pltpu.SemaphoreType.DMA((1,)),
            pltpu.SemaphoreType.DMA((4,)),
            pltpu.SemaphoreType.DMA,
        ],
        compiler_params=params(14),
        name="own_rows",
    )(
        pre_len,
        *stay(
            win_len, gates, pre_gate.reshape(16, 128), qkv, head_gain,
            pre_kv[0], win_cache, state_cache[:, 0],
        )
    )

    partial, pack = pl.pallas_call(
        guest_kernel,
        out_shape=(jax.ShapeDtypeStruct((16, 8, 128), F32), jax.ShapeDtypeStruct((8, 128), F32)),
        in_specs=[SMEM] + [VMEM] * 4 + [HBM] + [VMEM] * 2,
        out_specs=(VMEM, VMEM),
        scratch_shapes=[pltpu.VMEM((2, 128), F32), pltpu.SemaphoreType.DMA],
        compiler_params=params(8),
        name="guest",
    )(pre_len, message, got, own_heads, fresh_state, *stay(head_gain), pre_kv[0], out_weight)

    expert_in = w_in[0].reshape(2048, 2, 4, 128).transpose(0, 2, 1, 3).reshape(16384, 128)
    total = partial
    for axis in ("x", "y", "z"):
        parts = [swap(total, axis, flip) for flip in (1, 2, 3)]
        total = (total + parts[0]) + (parts[1] + parts[2])
    packet = pl.pallas_call(
        hidden_kernel,
        out_shape=jax.ShapeDtypeStruct((256, 128), BF16),
        in_specs=[VMEM] * 5,
        out_specs=VMEM,
        compiler_params=params(2),
        name="hidden",
    )(total, message, got, resid, fresh_state)
    packet, pack = lax.optimization_barrier((packet, pack))
    theirs = swap(packet, "s", 1)
    next_door = swap(pack, "t", 1)
    router_near, in_near = pl.pallas_call(
        fetch_kernel,
        out_shape=(pltpu.VMEM((2048, 128), BF16), pltpu.VMEM((8192, 128), BF16)),
        in_specs=[ANY] + [HBM] * 2,
        out_specs=(VMEM,) * 2,
        scratch_shapes=[pltpu.SemaphoreType.DMA((3,))],
        compiler_params=params(2),
        name="fetch",
    )(packet, *stay(router, expert_in))

    beyond = swap(packet, "t", 1)
    order, chooser, member, spread, use = pl.pallas_call(
        prepare_kernel,
        out_shape=(
            jax.ShapeDtypeStruct((32, 32), F32),
            jax.ShapeDtypeStruct((8, 32), F32),
            jax.ShapeDtypeStruct((32, 128), F32),
            jax.ShapeDtypeStruct((128, 1024), BF16),
            jax.ShapeDtypeStruct((32, 256), F32),
        ),
        in_specs=[VMEM] * 3,
        out_specs=(VMEM,) * 5,
        compiler_params=params(4),
        name="prepare",
    )(pack, next_door, routes.T)
    theirs, router_near, in_near, order, chooser, member, spread, use = lax.optimization_barrier(
        (theirs, router_near, in_near, order, chooser, member, spread, use)
    )
    cross = swap(theirs, "t", 1)
    term, own = pl.pallas_call(
        expert_kernel,
        out_shape=(jax.ShapeDtypeStruct((256, 128), F32), jax.ShapeDtypeStruct((8, 128), F32)),
        in_specs=[VMEM] * 11 + [HBM] * 2,
        out_specs=(VMEM, VMEM),
        scratch_shapes=[
            pltpu.VMEM((16, 8, 128), F32),
            pltpu.VMEM((8192, 128), BF16),
            pltpu.VMEM((512, 2048), BF16),
            pltpu.SemaphoreType.DMA((4,)),
            pltpu.SemaphoreType.DMA((4,)),
        ],
        compiler_params=params(12),
        name="experts",
    )(
        order, chooser, member, spread, moe_gain.reshape(1, 2048), packet, theirs, beyond, cross,
        router_near, in_near, *stay(expert_in, w_down[0]),
    )
    back = lax.all_to_all(term.reshape(256, 1, 128), ("s", "t", "z", "y", "x"), 0, 0, tiled=True)
    layer_out = pl.pallas_call(
        finish_kernel,
        out_shape=jax.ShapeDtypeStruct((8, 32), BF16),
        in_specs=[VMEM] * 3,
        out_specs=VMEM,
        compiler_params=params(2),
        name="finish",
    )(use, back.reshape(256, 128), own)

    late_qkv, late_gate, late_state, late_pack, _ = lax.optimization_barrier(
        (dec_qkv, dec_gate, state_cache, pack, own)
    )
    taken = jnp.arange(8, dtype=F32) == late_pack[0, :8]
    previous = jnp.where(taken[:, None, None], theirs[None, 128:], late_state[:, 0]).astype(F32)
    own_k, own_v = late_qkv[:, 1].astype(F32), late_qkv[:, 2].astype(F32)
    states = jnp.exp(late_gate)[:, :, None] * previous + own_k[:, :, None] * own_v[:, None, :]
    return layer_out, states[:, None]


def solution(mesh):
    fine = Mesh(mesh.devices.reshape(2, 4, 4, 4, 2), ("s", "y", "x", "z", "t"))
    placed = (
        P(BLOCKS, None, None, GRID),
        P(BLOCKS, GRID, None),
        P(BLOCKS),
        P(BLOCKS),
        P(BLOCKS),
        P(BLOCKS, None, GRID),
        P(BLOCKS, GRID),
        P(BLOCKS, GRID, None, None),
        P(BLOCKS, None, None, GRID),
        P(None, GRID),
        P(GRID, None),
        P(BLOCKS, None),
        P(),
        P(),
        P(),
        P(("s",) + GRID, None, None, "t"),
        P(("s",) + GRID, "t", None),
    )
    return jax.shard_map(
        on_device,
        mesh=fine,
        in_specs=placed,
        out_specs=(P(BLOCKS, GRID), P(BLOCKS, GRID, None, None)),
        check_vma=False,
    )
```

```python
import jax
import jax.numpy as jnp
from jax import lax
from jax.experimental import pallas as pl
from jax.experimental.pallas import tpu as pltpu
from jax.sharding import Mesh, PartitionSpec as P

GRID = ("y", "x", "z")
BLOCKS = ("s", "t")
F32 = jnp.float32
BF16 = jnp.bfloat16
EXACT = lax.Precision.HIGHEST
SCALE = 128 ** (-0.5)

ANY = pl.BlockSpec(memory_space=pl.ANY)
HBM = pl.BlockSpec(memory_space=pl.ANY)
VMEM = pl.BlockSpec(memory_space=pltpu.VMEM)
SMEM = pl.BlockSpec(memory_space=pltpu.SMEM)


def params(mib):
    return pltpu.CompilerParams(vmem_limit_bytes=int(mib * 1024 * 1024))


def stay(*arrays):
    return [pltpu.with_memory_space_constraint(a, pltpu.HBM) for a in arrays]


def swap(shard, axis, flip):
    return lax.ppermute(shard, axis, [(i, i ^ flip) for i in range(lax.axis_size(axis))])


def iota(shape, axis):
    return lax.broadcasted_iota(jnp.int32, shape, axis)


def norm_rows(values, gain_row):
    return values * lax.rsqrt(jnp.mean(values * values, axis=-1, keepdims=True) + 1e-06) * gain_row


def dot(a, b, precision=None):
    return jnp.dot(a, b, preferred_element_type=F32, precision=precision)


def dot_t(a, b):
    return lax.dot_general(a, b, (((1,), (1,)), ((), ())), preferred_element_type=F32)


def beside(*parts):
    return jnp.concatenate(parts, axis=1)


def split_rows(queries):
    odd = iota((8, 128), 0) % 2 == 1
    return beside(jnp.where(odd, 0.0, queries), jnp.where(odd, queries, 0.0)).astype(BF16)


def own_block():
    return lax.axis_index("s") * 2 + lax.axis_index("t")


def picked(rows, index):
    return jnp.sum(jnp.where(iota(rows.shape, 0) == index, rows, 0.0), axis=0, keepdims=True)


def message_kernel(owner_hbm, gate_hbm, qkv_hbm, resid_hbm, out_ref, owner_ref, gate_ref, qkv_ref, resid_ref, sems):
    pairs = [(owner_hbm, owner_ref), (gate_hbm, gate_ref), (qkv_hbm, qkv_ref), (resid_hbm, resid_ref)]
    copies = [pltpu.make_async_copy(a, b, sems.at[i]) for i, (a, b) in enumerate(pairs)]
    for copy in copies:
        copy.start()
    for copy in copies:
        copy.wait()
    owner = owner_ref[...]
    for part in range(3):
        out_ref[part : part + 1, :] = picked(qkv_ref[part].astype(F32), owner)
    gate = jnp.sum(jnp.where(iota((1, 8), 1) == owner, gate_ref[...], 0.0), axis=1, keepdims=True)
    out_ref[3:4, :] = jnp.broadcast_to(gate, (1, 128))
    out_ref[4:8, :] = jnp.broadcast_to(owner.astype(F32), (4, 128))
    row = picked(resid_ref[...].astype(F32), owner)
    for c in range(16):
        out_ref[8 + c : 9 + c, :] = row[:, c * 128 : (c + 1) * 128]


def own_rows_kernel(
    length_ref, live_hbm, gate_hbm, decay_hbm, qkv_hbm, gain_hbm, kv_hbm, cache_hbm, state_hbm,
    head_ref, fresh_ref, live_ref, gate_ref, decay_ref, qkv_ref, gain_ref, kv_ref, cache_ref, state_ref,
    small_sem, kv_sem, cache_sem, state_sem,
):
    small = [
        (decay_hbm, decay_ref), (qkv_hbm, qkv_ref), (live_hbm, live_ref),
        (gate_hbm, gate_ref), (gain_hbm, gain_ref),
    ]
    small_copies = [pltpu.make_async_copy(a, b, small_sem.at[i]) for i, (a, b) in enumerate(small)]
    kv_copies = [pltpu.make_async_copy(kv_hbm, kv_ref, kv_sem.at[0])]
    state_copy = pltpu.make_async_copy(state_hbm, state_ref, state_sem)
    cache_copies = [
        pltpu.make_async_copy(cache_hbm.at[pl.ds(2 * p, 2)], cache_ref.at[pl.ds(2 * p, 2)], cache_sem.at[p]) for p in range(4)
    ]
    for copy in small_copies + kv_copies + cache_copies + [state_copy]:
        copy.start()

    for copy in small_copies:
        copy.wait()
    length = length_ref[0]
    places = iota((16, 128), 0) * 128 + iota((16, 128), 1)
    kept = jnp.where(places < length, decay_ref[...], 0.0)
    later = (iota((128, 128), 0) > iota((128, 128), 1)).astype(F32)
    later_rows = (iota((16, 16), 1) > iota((16, 16), 0)).astype(F32)
    totals = jnp.broadcast_to(jnp.sum(kept, axis=1, keepdims=True), (16, 128))
    suffix = dot(kept, later, EXACT) + dot(later_rows, totals, EXACT)
    weights = jnp.where(places < length, jnp.exp(suffix), 0.0)

    for copy in kv_copies:
        copy.wait()
    fresh = jnp.zeros((128, 128), F32)
    for i in range(8):
        parts = []
        for j in (2 * i, 2 * i + 1):
            turned = kv_ref[0, j * 128 : (j + 1) * 128, :].T.astype(F32)
            parts.append((turned * weights[j : j + 1, :]).astype(BF16))
        fresh += dot(beside(*parts), kv_ref[1, i * 256 : (i + 1) * 256, :])
    fresh_ref[...] = fresh.astype(BF16)

    queries = qkv_ref[0]
    q32, k32, v32 = queries.astype(F32), qkv_ref[1].astype(F32), qkv_ref[2].astype(F32)
    self_raw = jnp.sum(q32 * k32, axis=1, keepdims=True)
    self_score = self_raw * SCALE
    scores = jnp.zeros((8, 1024), F32)
    live = jnp.zeros((8, 1024), jnp.int32)
    gate = jnp.zeros((8, 128), F32)
    halves = split_rows(q32)
    for r in range(8):
        live = jnp.where(iota((8, 1024), 0) == r, live_ref[r], live)
        gate = jnp.where(iota((8, 128), 0) == r, gate_ref[r], gate)
    for p in range(4):
        cache_copies[p].wait()
        both = dot_t(halves, beside(cache_ref[2 * p, 0], cache_ref[2 * p + 1, 0]))
        scores = jnp.where(iota((8, 1024), 0) // 2 == p, both, scores)
    scores = scores * SCALE
    alive = iota((8, 1024), 1) >= 1024 - live
    peak = jnp.max(jnp.where(alive, scores, -jnp.inf), axis=1, keepdims=True)
    peak = jnp.maximum(peak, self_score)
    prob = jnp.where(alive, jnp.exp(scores - peak), 0.0).astype(BF16)
    self_prob = jnp.exp(self_score - peak).astype(BF16).astype(F32)
    below = jnp.sum(prob.astype(F32), axis=1, keepdims=True) + self_prob
    above = jnp.zeros((8, 128), F32)
    linear = jnp.zeros((8, 128), F32)
    state_copy.wait()
    row = iota((8, 128), 0)
    for p in range(4):
        both = dot(prob, beside(cache_ref[2 * p, 1], cache_ref[2 * p + 1, 1]))
        above = jnp.where(row == 2 * p, both[:, :128], jnp.where(row == 2 * p + 1, both[:, 128:], above))
    for p in range(2):
        a, b, c, d = (state_ref[4 * p + i] for i in range(4))
        both = dot(halves, jnp.concatenate([beside(a, c), beside(b, d)], axis=0))
        linear = jnp.where(row // 2 == 2 * p, both[:, :128], jnp.where(row // 2 == 2 * p + 1, both[:, 128:], linear))
    window_out = (above + self_prob * v32) / below
    linear_out = jnp.exp(gate) * linear + self_raw * v32
    head_ref[...] = norm_rows(linear_out, gain_ref[0:1, :]) + norm_rows(window_out, gain_ref[1:2, :])


def guest_kernel(
    length_ref, message_ref, got_ref, head_ref, fresh_ref, gain_hbm, kv_ref, weight_ref,
    out_ref, pack_ref, gain_ref, gain_sem,
):
    gain_copy = pltpu.make_async_copy(gain_hbm, gain_ref, gain_sem)
    gain_copy.start()
    owner = message_ref[4:5, :]
    rows = iota((8, 128), 0).astype(F32)
    pack_ref[...] = jnp.where(rows == 0.0, owner, got_ref[4:5, :])
    q32, k32, v32 = got_ref[0:1, :], got_ref[1:2, :], got_ref[2:3, :]
    self_raw = jnp.sum(q32 * k32, axis=1, keepdims=True)
    self_score = self_raw * SCALE
    query = jnp.broadcast_to(q32, (8, 128))
    linear_out = jnp.exp(got_ref[3:4, :]) * dot(query.astype(BF16), fresh_ref[...])[0:1, :] + self_raw * v32

    scores = dot_t(split_rows(query), beside(kv_ref[0, 0:1024, :], kv_ref[0, 1024:2048, :])) * SCALE
    places = iota((8, 1024), 1) + iota((8, 1024), 0) % 2 * 1024
    length = length_ref[0]
    alive = (places < length) & (places >= length - 1024)
    peak = jnp.max(jnp.where(alive, scores, -jnp.inf), axis=1, keepdims=True)
    peak = jnp.maximum(jnp.maximum(peak[0:1, :], peak[1:2, :]), self_score)
    prob = jnp.where(alive, jnp.exp(scores - peak), 0.0).astype(BF16)
    self_prob = jnp.exp(self_score - peak).astype(BF16).astype(F32)
    total = jnp.sum(prob.astype(F32), axis=1, keepdims=True)
    below = total[0:1, :] + total[1:2, :] + self_prob
    both = dot(prob, beside(kv_ref[1, 0:1024, :], kv_ref[1, 1024:2048, :]))
    window_out = (both[0:1, :128] + both[1:2, 128:] + self_prob * v32) / below
    gain_copy.wait()
    head = norm_rows(linear_out, gain_ref[0:1, :]) + norm_rows(window_out, gain_ref[1:2, :])
    head = jnp.where(rows == owner, head, head_ref[...]).astype(BF16)
    for c in range(8):
        part = dot(head, weight_ref[:, c * 256 : (c + 1) * 256])
        out_ref[2 * c] = part[:, :128]
        out_ref[2 * c + 1] = part[:, 128:]


def named_by(turned_ref):
    turned = turned_ref[...]
    experts = iota((128, 32), 0)
    member = jnp.zeros((128, 32), F32)
    for k in range(8):
        member = jnp.where(turned[k : k + 1, :] == experts, 1.0, member)
    same = (iota((32, 32), 0) == iota((32, 32), 1)).astype(F32)
    return dot_t(same, member)


def own_expert():
    return lax.axis_index("s") * 64 + lax.axis_index("y") * 16 + lax.axis_index("x") * 4 + lax.axis_index("z")


def prepare_kernel(
    pack_ref, beside_ref, turned_ref, own_rows_ref, chooser_ref, member_ref, spread_ref, use_ref
):
    block = own_block()
    owners = [pack_ref[0, 0], pack_ref[1, 0], beside_ref[0, 0], beside_ref[1, 0]]
    blocks = [block, block ^ 2, block ^ 1, block ^ 3]
    ids = iota((32, 32), 1)
    place, row = ids // 8, (ids % 8).astype(F32)
    target = jnp.zeros((32, 32), F32)
    for j in range(4):
        own = (blocks[j] * 8).astype(F32) + row
        other = (blocks[j ^ 1] * 8).astype(F32) + owners[j ^ 1]
        target = jnp.where(place == j, jnp.where(row == owners[j], other, own), target)
    order = (target == iota((32, 32), 0).astype(F32)).astype(F32)

    expert = own_expert()
    names_own = jnp.max((turned_ref[...] == expert).astype(F32), axis=0, keepdims=True)
    names_own = jnp.broadcast_to(names_own, (8, 32))
    upper = (iota((32, 32), 0) < iota((32, 32), 1)).astype(F32)
    rank = dot(names_own, upper)
    slots = (iota((8, 32), 0) % 4).astype(F32)
    chooser = jnp.where(names_own > 0, (rank == slots).astype(F32), 0.0)
    gathered = dot(chooser, order)
    member = named_by(turned_ref)
    member_ref[...] = dot(chooser, member)

    tile_row = iota((32, 64), 1) // 16 * 8 + iota((32, 64), 1) % 8
    widen = (tile_row == iota((32, 64), 0)).astype(F32)
    wide = dot(gathered, widen)
    odd = iota((8, 64), 1) // 8 % 2 == 1
    chooser_ref[...] = jnp.concatenate([jnp.where(odd, 0.0, wide), jnp.where(odd, wide, 0.0)], axis=0).astype(BF16)
    first = (iota((8, 32), 1) == iota((8, 32), 0) + block * 8).astype(F32)
    own_wide = dot(dot(first, order), widen)
    tile = lax.axis_index("y") * 4 + lax.axis_index("x")
    own_rows_ref[...] = jnp.where(odd == (tile % 2 == 1), own_wide, 0.0).astype(BF16)
    spread_ref[...] = (iota((128, 1024), 1) // 8 == iota((128, 1024), 0)).astype(BF16)

    lower = (iota((32, 32), 1) < iota((32, 32), 0)).astype(F32)
    slot = jnp.where(member > 0, dot(lower, member), -1.0)
    first = (iota((8, 32), 1) == iota((8, 32), 0) + block * 8).astype(F32)
    slot = dot(first, slot)
    src = iota((128, 256), 1)
    sender = src // 128 * 64 + src % 16 * 4 + src // 16 % 4
    slot = dot(slot, (sender == iota((128, 256), 0)).astype(F32))
    for k in range(4):
        use_ref[k * 8 : (k + 1) * 8, :] = (slot == float(k)).astype(F32)


def fetch_kernel(after_ref, router_hbm, in_hbm, down_hbm, router_ref, in_ref, down_ref, sems):
    pairs = [(router_hbm, router_ref, 1), (in_hbm, in_ref, 8), (down_hbm, down_ref, 4)]
    copies = []
    for source, target, cuts in pairs:
        rows = source.shape[0] // cuts
        for i in range(cuts):
            part = pl.ds(i * rows, rows)
            copies.append(pltpu.make_async_copy(source.at[part], target.at[part], sems.at[len(copies)]))
    for copy in copies:
        copy.start()
    for copy in copies:
        copy.wait()


def sum_kernel(two_ref, three_ref, one_ref, total_ref, out_ref):
    out_ref[...] = (total_ref[...] + one_ref[...]) + (two_ref[...] + three_ref[...])


def hidden_kernel(three_ref, two_ref, one_ref, total_ref, message_ref, got_ref, resid_ref, fresh_ref, out_ref):
    taken = iota((8, 128), 0).astype(F32) == message_ref[4:5, :]
    for pair in range(8):
        parts = []
        for c in (2 * pair, 2 * pair + 1):
            rows = resid_ref[:, c * 128 : (c + 1) * 128].astype(F32)
            total = (total_ref[c] + one_ref[c]) + (two_ref[c] + three_ref[c])
            parts.append(jnp.where(taken, got_ref[8 + c : 9 + c, :], rows) + total)
        out_ref[pair * 16 : (pair + 1) * 16, :] = jnp.concatenate(parts, axis=0).astype(BF16)
    out_ref[128:256, :] = fresh_ref[...]


def expert_kernel(
    own_rows_ref, chooser_ref, member_ref, spread_ref, gain_ref, packet_ref, theirs_ref, next_ref, cross_ref,
    router_ref, in_ref, down_ref, out_ref, own_ref, turn_ref,
):
    expert = own_expert()
    packets = (packet_ref, theirs_ref, next_ref, cross_ref)

    right = beside(*(jnp.concatenate([ref[p * 16 : (p + 1) * 16, :] for ref in packets], axis=0) for p in range(8)))
    both = dot(chooser_ref[...], right)
    tiles = [both[c % 2 * 8 : c % 2 * 8 + 8, c // 2 * 128 : (c // 2 + 1) * 128] for c in range(16)]
    squares = tiles[0] * tiles[0]
    for x in tiles[1:]:
        squares += x * x
    scale = lax.rsqrt(jnp.sum(squares, axis=1, keepdims=True) * (1.0 / 2048) + 1e-06)
    tiles = [x * scale * gain_ref[:, c * 128 : (c + 1) * 128] for c, x in enumerate(tiles)]

    logits = dot(beside(*tiles).astype(BF16), router_ref[...])
    member = member_ref[...]
    chosen = jnp.where(member > 0, 1.0 / (1.0 + jnp.exp(-logits)), 0.0)
    share = jnp.sum(jnp.where(iota((8, 128), 1) == expert, chosen, 0.0), axis=1, keepdims=True)
    share = share / jnp.sum(chosen, axis=1, keepdims=True)
    gates = jnp.where(jnp.sum(member, axis=1, keepdims=True) > 0, share, 0.0)

    stacked = jnp.concatenate(tiles, axis=0)
    repeated = dot(stacked.astype(BF16), spread_ref[...])
    kind = iota((8, 1024), 1) % 8 - iota((8, 1024), 0) // 4
    pre = jnp.zeros((64, 256), F32)
    for c in range(8):
        halves = [repeated[i * 8 : (i + 1) * 8, :] for i in (c, c + 8)]
        left = jnp.concatenate([jnp.where(kind == 2 * p, half, 0.0) for half in halves for p in range(4)], axis=0)
        right = beside(in_ref[c * 1024 : (c + 1) * 1024, :], in_ref[(c + 8) * 1024 : (c + 9) * 1024, :])
        pre += dot(left.astype(BF16), right)
    pre = pre[:32, :128] + pre[32:, 128:]
    acts = []
    for p in range(4):
        both = pre[p * 8 : (p + 1) * 8, :]
        acts.append(both / (1.0 + jnp.exp(-both)) * pltpu.roll(both, 4, 0))
    act = jnp.concatenate(acts, axis=1).astype(BF16)
    for c in range(8):
        part = dot(act, down_ref[:, c * 256 : (c + 1) * 256])
        turn_ref[2 * c] = part[:, :128] * gates
        turn_ref[2 * c + 1] = part[:, 128:] * gates

    lane_block = iota((16, 128), 1) // 32
    by_slot = [turn_ref[:, k, :] for k in range(4)]
    for q in range(4):
        piece = jnp.zeros((16, 128), F32)
        for k in range(4):
            shift = (k - q) * 32 % 128
            moved = by_slot[k] if shift == 0 else pltpu.roll(by_slot[k], shift, 1)
            piece = jnp.where(lane_block == k, moved, piece)
        for b in range(4):
            out_ref[b * 64 + q * 16 : b * 64 + (q + 1) * 16, :] = piece

    tile = lax.axis_index("y") * 4 + lax.axis_index("x")
    rows = pl.ds(pl.multiple_of(tile // 2 * 16, 16), 16)
    mine = dot(own_rows_ref[...], jnp.concatenate([ref[rows, :] for ref in packets], axis=0))
    deep = lax.axis_index("z")
    own = mine
    for q in range(1, 4):
        own = jnp.where(deep == q, pltpu.roll(mine, 128 - q * 32, 1), own)
    own_ref[...] = own


def finish_kernel(use_ref, back_ref, own_ref, out_ref):
    back = back_ref[...]
    high = back.astype(BF16)
    low = (back - high.astype(F32)).astype(BF16)
    use = use_ref[...].astype(BF16)
    total = dot(use, high) + dot(use, low)
    out = own_ref[:, 0:32]
    for k in range(4):
        out += total[k * 8 : (k + 1) * 8, k * 32 : (k + 1) * 32]
    out_ref[...] = out.astype(BF16)


def on_device(
    pre_kv, pre_gate, pre_len, owners, win_len, dec_qkv, dec_gate, state_cache, win_cache,
    head_gain, out_weight, resid, moe_gain, router, routes, w_in, w_down,
):
    qkv = dec_qkv.transpose(1, 0, 2)
    gates = dec_gate.reshape(8)

    message = pl.pallas_call(
        message_kernel,
        out_shape=jax.ShapeDtypeStruct((24, 128), F32),
        in_specs=[ANY] + [HBM] * 3,
        out_specs=VMEM,
        scratch_shapes=[
            pltpu.VMEM((1, 1), jnp.int32),
            pltpu.VMEM((1, 8), F32),
            pltpu.VMEM((3, 8, 128), BF16),
            pltpu.VMEM((8, 2048), BF16),
            pltpu.SemaphoreType.DMA((4,)),
        ],
        compiler_params=params(2),
        name="message",
    )(owners.reshape(1, 1), *stay(gates.reshape(1, 8), qkv, resid))
    got = swap(message, "s", 1)

    own_heads, fresh_state = pl.pallas_call(
        own_rows_kernel,
        out_shape=(jax.ShapeDtypeStruct((8, 128), F32), jax.ShapeDtypeStruct((128, 128), BF16)),
        in_specs=[SMEM] + [HBM] * 8,
        out_specs=(VMEM, VMEM),
        scratch_shapes=[
            pltpu.SMEM((8,), jnp.int32),
            pltpu.SMEM((8,), F32),
            pltpu.VMEM((16, 128), F32),
            pltpu.VMEM((3, 8, 128), BF16),
            pltpu.VMEM((2, 128), F32),
            pltpu.VMEM((2, 2048, 128), BF16),
            pltpu.VMEM((8, 2, 1024, 128), BF16),
            pltpu.VMEM((8, 128, 128), BF16),
            pltpu.SemaphoreType.DMA((5,)),
            pltpu.SemaphoreType.DMA((1,)),
            pltpu.SemaphoreType.DMA((4,)),
            pltpu.SemaphoreType.DMA,
        ],
        compiler_params=params(14),
        name="own_rows",
    )(
        pre_len,
        *stay(
            win_len, gates, pre_gate.reshape(16, 128), qkv, head_gain,
            pre_kv[0], win_cache, state_cache[:, 0],
        )
    )

    partial, pack = pl.pallas_call(
        guest_kernel,
        out_shape=(jax.ShapeDtypeStruct((16, 8, 128), F32), jax.ShapeDtypeStruct((8, 128), F32)),
        in_specs=[SMEM] + [VMEM] * 4 + [HBM] + [VMEM] * 2,
        out_specs=(VMEM, VMEM),
        scratch_shapes=[pltpu.VMEM((2, 128), F32), pltpu.SemaphoreType.DMA],
        compiler_params=params(8),
        name="guest",
    )(pre_len, message, got, own_heads, fresh_state, *stay(head_gain), pre_kv[0], out_weight)

    expert_in = w_in[0].reshape(2048, 2, 4, 128).transpose(0, 2, 1, 3).reshape(16384, 128)
    total = partial
    for axis in ("x", "y", "z"):
        parts = [swap(total, axis, flip) for flip in (1, 2, 3)]
        if axis != "z":
            total = pl.pallas_call(
                sum_kernel,
                out_shape=pltpu.VMEM((16, 8, 128), F32),
                in_specs=[VMEM] * 4,
                out_specs=VMEM,
                compiler_params=params(2),
                name="sum_" + axis,
            )(parts[1], parts[2], parts[0], total)
    packet = pl.pallas_call(
        hidden_kernel,
        out_shape=jax.ShapeDtypeStruct((256, 128), BF16),
        in_specs=[VMEM] * 8,
        out_specs=VMEM,
        compiler_params=params(2),
        name="hidden",
    )(*parts[::-1], total, message, got, resid, fresh_state)
    packet, pack = lax.optimization_barrier((packet, pack))
    theirs = swap(packet, "s", 1)
    next_door = swap(pack, "t", 1)
    router_near, in_near, down_near = pl.pallas_call(
        fetch_kernel,
        out_shape=(
            pltpu.VMEM((2048, 128), BF16),
            pltpu.VMEM((16384, 128), BF16),
            pltpu.VMEM((512, 2048), BF16),
        ),
        in_specs=[ANY] + [HBM] * 3,
        out_specs=(VMEM,) * 3,
        scratch_shapes=[pltpu.SemaphoreType.DMA((13,))],
        compiler_params=params(2),
        name="fetch",
    )(packet, *stay(router, expert_in, w_down[0]))

    beyond = swap(packet, "t", 1)
    own_rows, chooser, member, spread, use = pl.pallas_call(
        prepare_kernel,
        out_shape=(
            jax.ShapeDtypeStruct((8, 64), BF16),
            jax.ShapeDtypeStruct((16, 64), BF16),
            jax.ShapeDtypeStruct((8, 128), F32),
            jax.ShapeDtypeStruct((128, 1024), BF16),
            jax.ShapeDtypeStruct((32, 256), F32),
        ),
        in_specs=[VMEM] * 3,
        out_specs=(VMEM,) * 5,
        compiler_params=params(4),
        name="prepare",
    )(pack, next_door, routes.T)
    theirs, router_near, in_near, down_near, own_rows, chooser, member, spread, use = lax.optimization_barrier(
        (theirs, router_near, in_near, down_near, own_rows, chooser, member, spread, use)
    )
    cross = swap(theirs, "t", 1)
    term, own = pl.pallas_call(
        expert_kernel,
        out_shape=(jax.ShapeDtypeStruct((256, 128), F32), jax.ShapeDtypeStruct((8, 128), F32)),
        in_specs=[VMEM] * 12,
        out_specs=(VMEM, VMEM),
        scratch_shapes=[pltpu.VMEM((16, 8, 128), F32)],
        compiler_params=params(12),
        name="experts",
    )(
        own_rows, chooser, member, spread, moe_gain.reshape(1, 2048), packet, theirs, beyond, cross,
        router_near, in_near, down_near,
    )
    back = lax.all_to_all(term.reshape(256, 1, 128), ("s", "t", "z", "y", "x"), 0, 0, tiled=True)
    layer_out = pl.pallas_call(
        finish_kernel,
        out_shape=jax.ShapeDtypeStruct((8, 32), BF16),
        in_specs=[VMEM] * 3,
        out_specs=VMEM,
        compiler_params=params(2),
        name="finish",
    )(use, back.reshape(256, 128), own)

    late_qkv, late_gate, late_state, late_pack, _ = lax.optimization_barrier(
        (dec_qkv, dec_gate, state_cache, pack, own)
    )
    taken = jnp.arange(8, dtype=F32) == late_pack[0, :8]
    previous = jnp.where(taken[:, None, None], theirs[None, 128:], late_state[:, 0]).astype(F32)
    own_k, own_v = late_qkv[:, 1].astype(F32), late_qkv[:, 2].astype(F32)
    states = jnp.exp(late_gate)[:, :, None] * previous + own_k[:, :, None] * own_v[:, None, :]
    return layer_out, states[:, None]


def solution(mesh):
    fine = Mesh(mesh.devices.reshape(2, 4, 4, 4, 2), ("s", "y", "x", "z", "t"))
    placed = (
        P(BLOCKS, None, None, GRID),
        P(BLOCKS, GRID, None),
        P(BLOCKS),
        P(BLOCKS),
        P(BLOCKS),
        P(BLOCKS, None, GRID),
        P(BLOCKS, GRID),
        P(BLOCKS, GRID, None, None),
        P(BLOCKS, None, None, GRID),
        P(None, GRID),
        P(GRID, None),
        P(BLOCKS, None),
        P(),
        P(),
        P(),
        P(("s",) + GRID, None, None, "t"),
        P(("s",) + GRID, "t", None),
    )
    return jax.shard_map(
        on_device,
        mesh=fine,
        in_specs=placed,
        out_specs=(P(BLOCKS, GRID), P(BLOCKS, GRID, None, None)),
        check_vma=False,
    )
```

```python
import functools

import jax
import jax.numpy as jnp
from jax import lax
from jax.experimental import pallas as pl
from jax.experimental.pallas import tpu as pltpu
from jax.sharding import Mesh, PartitionSpec as P

GRID = ("y", "x", "z")
BLOCKS = ("s", "t")
F32 = jnp.float32
BF16 = jnp.bfloat16
EXACT = lax.Precision.HIGHEST
SCALE = 128 ** (-0.5)

ANY = pl.BlockSpec(memory_space=pl.ANY)
HBM = pl.BlockSpec(memory_space=pl.ANY)
VMEM = pl.BlockSpec(memory_space=pltpu.VMEM)
SMEM = pl.BlockSpec(memory_space=pltpu.SMEM)


def params(mib):
    return pltpu.CompilerParams(vmem_limit_bytes=int(mib * 1024 * 1024))


def stay(*arrays):
    return [pltpu.with_memory_space_constraint(a, pltpu.HBM) for a in arrays]


def swap(shard, axis, flip):
    return lax.ppermute(shard, axis, [(i, i ^ flip) for i in range(lax.axis_size(axis))])


def iota(shape, axis):
    return lax.broadcasted_iota(jnp.int32, shape, axis)


def norm_rows(values, gain_row):
    return values * lax.rsqrt(jnp.mean(values * values, axis=-1, keepdims=True) + 1e-06) * gain_row


def dot(a, b, precision=None):
    return jnp.dot(a, b, preferred_element_type=F32, precision=precision)


def dot_t(a, b):
    return lax.dot_general(a, b, (((1,), (1,)), ((), ())), preferred_element_type=F32)


def beside(*parts):
    return jnp.concatenate(parts, axis=1)


def split_rows(queries):
    odd = iota((8, 128), 0) % 2 == 1
    return beside(jnp.where(odd, 0.0, queries), jnp.where(odd, queries, 0.0)).astype(BF16)


def own_block():
    return lax.axis_index("s") * 2 + lax.axis_index("t")


def picked(rows, index):
    return jnp.sum(jnp.where(iota(rows.shape, 0) == index, rows, 0.0), axis=0, keepdims=True)


def message_kernel(owner_hbm, gate_hbm, qkv_hbm, resid_hbm, out_ref, owner_ref, gate_ref, qkv_ref, resid_ref, sems):
    pairs = [(owner_hbm, owner_ref), (gate_hbm, gate_ref), (qkv_hbm, qkv_ref), (resid_hbm, resid_ref)]
    copies = [pltpu.make_async_copy(a, b, sems.at[i]) for i, (a, b) in enumerate(pairs)]
    for copy in copies:
        copy.start()
    for copy in copies:
        copy.wait()
    owner = owner_ref[...]
    for part in range(3):
        out_ref[part : part + 1, :] = picked(qkv_ref[part].astype(F32), owner)
    gate = jnp.sum(jnp.where(iota((1, 8), 1) == owner, gate_ref[...], 0.0), axis=1, keepdims=True)
    out_ref[3:4, :] = jnp.broadcast_to(gate, (1, 128))
    out_ref[4:8, :] = jnp.broadcast_to(owner.astype(F32), (4, 128))
    row = picked(resid_ref[...].astype(F32), owner)
    for c in range(16):
        out_ref[8 + c : 9 + c, :] = row[:, c * 128 : (c + 1) * 128]


def own_rows_kernel(
    length_ref, live_hbm, gate_hbm, decay_hbm, qkv_hbm, gain_hbm, kv_hbm, cache_hbm, state_hbm,
    head_ref, fresh_ref, live_ref, gate_ref, decay_ref, qkv_ref, gain_ref, kv_ref, cache_ref, state_ref,
    small_sem, kv_sem, cache_sem, state_sem,
):
    small = [
        (decay_hbm, decay_ref), (qkv_hbm, qkv_ref), (live_hbm, live_ref),
        (gate_hbm, gate_ref), (gain_hbm, gain_ref),
    ]
    small_copies = [pltpu.make_async_copy(a, b, small_sem.at[i]) for i, (a, b) in enumerate(small)]
    kv_copies = [pltpu.make_async_copy(kv_hbm, kv_ref, kv_sem.at[0])]
    state_copy = pltpu.make_async_copy(state_hbm, state_ref, state_sem)
    cache_copies = [
        pltpu.make_async_copy(cache_hbm.at[pl.ds(2 * p, 2)], cache_ref.at[pl.ds(2 * p, 2)], cache_sem.at[p]) for p in range(4)
    ]
    for copy in small_copies + kv_copies + cache_copies + [state_copy]:
        copy.start()

    for copy in small_copies:
        copy.wait()
    length = length_ref[0]
    places = iota((16, 128), 0) * 128 + iota((16, 128), 1)
    kept = jnp.where(places < length, decay_ref[...], 0.0)
    later = (iota((128, 128), 0) > iota((128, 128), 1)).astype(F32)
    later_rows = (iota((16, 16), 1) > iota((16, 16), 0)).astype(F32)
    totals = jnp.broadcast_to(jnp.sum(kept, axis=1, keepdims=True), (16, 128))
    suffix = dot(kept, later, EXACT) + dot(later_rows, totals, EXACT)
    weights = jnp.where(places < length, jnp.exp(suffix), 0.0)

    for copy in kv_copies:
        copy.wait()
    fresh = jnp.zeros((128, 128), F32)
    for i in range(8):
        parts = []
        for j in (2 * i, 2 * i + 1):
            turned = kv_ref[0, j * 128 : (j + 1) * 128, :].T.astype(F32)
            parts.append((turned * weights[j : j + 1, :]).astype(BF16))
        fresh += dot(beside(*parts), kv_ref[1, i * 256 : (i + 1) * 256, :])
    fresh_ref[...] = fresh.astype(BF16)

    queries = qkv_ref[0]
    q32, k32, v32 = queries.astype(F32), qkv_ref[1].astype(F32), qkv_ref[2].astype(F32)
    self_raw = jnp.sum(q32 * k32, axis=1, keepdims=True)
    self_score = self_raw * SCALE
    scores = jnp.zeros((8, 1024), F32)
    live = jnp.zeros((8, 1024), jnp.int32)
    gate = jnp.zeros((8, 128), F32)
    halves = split_rows(q32)
    for r in range(8):
        live = jnp.where(iota((8, 1024), 0) == r, live_ref[r], live)
        gate = jnp.where(iota((8, 128), 0) == r, gate_ref[r], gate)
    for p in range(4):
        cache_copies[p].wait()
        both = dot_t(halves, beside(cache_ref[2 * p, 0], cache_ref[2 * p + 1, 0]))
        scores = jnp.where(iota((8, 1024), 0) // 2 == p, both, scores)
    scores = scores * SCALE
    alive = iota((8, 1024), 1) >= 1024 - live
    peak = jnp.max(jnp.where(alive, scores, -jnp.inf), axis=1, keepdims=True)
    peak = jnp.maximum(peak, self_score)
    prob = jnp.where(alive, jnp.exp(scores - peak), 0.0).astype(BF16)
    self_prob = jnp.exp(self_score - peak).astype(BF16).astype(F32)
    below = jnp.sum(prob.astype(F32), axis=1, keepdims=True) + self_prob
    above = jnp.zeros((8, 128), F32)
    linear = jnp.zeros((8, 128), F32)
    state_copy.wait()
    row = iota((8, 128), 0)
    for p in range(4):
        both = dot(prob, beside(cache_ref[2 * p, 1], cache_ref[2 * p + 1, 1]))
        above = jnp.where(row == 2 * p, both[:, :128], jnp.where(row == 2 * p + 1, both[:, 128:], above))
    for p in range(2):
        a, b, c, d = (state_ref[4 * p + i] for i in range(4))
        both = dot(halves, jnp.concatenate([beside(a, c), beside(b, d)], axis=0))
        linear = jnp.where(row // 2 == 2 * p, both[:, :128], jnp.where(row // 2 == 2 * p + 1, both[:, 128:], linear))
    window_out = (above + self_prob * v32) / below
    linear_out = jnp.exp(gate) * linear + self_raw * v32
    head_ref[...] = norm_rows(linear_out, gain_ref[0:1, :]) + norm_rows(window_out, gain_ref[1:2, :])


def guest_kernel(
    length_ref, message_ref, got_ref, head_ref, fresh_ref, gain_hbm, kv_ref, weight_ref,
    out_ref, pack_ref, gain_ref, gain_sem,
):
    gain_copy = pltpu.make_async_copy(gain_hbm, gain_ref, gain_sem)
    gain_copy.start()
    owner = message_ref[4:5, :]
    rows = iota((8, 128), 0).astype(F32)
    pack_ref[...] = jnp.where(rows == 0.0, owner, got_ref[4:5, :])
    q32, k32, v32 = got_ref[0:1, :], got_ref[1:2, :], got_ref[2:3, :]
    self_raw = jnp.sum(q32 * k32, axis=1, keepdims=True)
    self_score = self_raw * SCALE
    query = jnp.broadcast_to(q32, (8, 128))
    linear_out = jnp.exp(got_ref[3:4, :]) * dot(query.astype(BF16), fresh_ref[...])[0:1, :] + self_raw * v32

    scores = dot_t(split_rows(query), beside(kv_ref[0, 0:1024, :], kv_ref[0, 1024:2048, :])) * SCALE
    places = iota((8, 1024), 1) + iota((8, 1024), 0) % 2 * 1024
    length = length_ref[0]
    alive = (places < length) & (places >= length - 1024)
    peak = jnp.max(jnp.where(alive, scores, -jnp.inf), axis=1, keepdims=True)
    peak = jnp.maximum(jnp.maximum(peak[0:1, :], peak[1:2, :]), self_score)
    prob = jnp.where(alive, jnp.exp(scores - peak), 0.0).astype(BF16)
    self_prob = jnp.exp(self_score - peak).astype(BF16).astype(F32)
    total = jnp.sum(prob.astype(F32), axis=1, keepdims=True)
    below = total[0:1, :] + total[1:2, :] + self_prob
    both = dot(prob, beside(kv_ref[1, 0:1024, :], kv_ref[1, 1024:2048, :]))
    window_out = (both[0:1, :128] + both[1:2, 128:] + self_prob * v32) / below
    gain_copy.wait()
    head = norm_rows(linear_out, gain_ref[0:1, :]) + norm_rows(window_out, gain_ref[1:2, :])
    head = jnp.where(rows == owner, head, head_ref[...]).astype(BF16)
    for c in range(8):
        part = dot(head, weight_ref[:, c * 256 : (c + 1) * 256])
        out_ref[2 * c] = part[:, :128]
        out_ref[2 * c + 1] = part[:, 128:]


def named_by(turned_ref):
    turned = turned_ref[...]
    experts = iota((128, 32), 0)
    member = jnp.zeros((128, 32), F32)
    for k in range(8):
        member = jnp.where(turned[k : k + 1, :] == experts, 1.0, member)
    same = (iota((32, 32), 0) == iota((32, 32), 1)).astype(F32)
    return dot_t(same, member)


def own_expert():
    return lax.axis_index("s") * 64 + lax.axis_index("y") * 16 + lax.axis_index("x") * 4 + lax.axis_index("z")


def prepare_kernel(
    pack_ref, beside_ref, turned_ref, own_rows_ref, chooser_ref, member_ref, spread_ref, use_ref
):
    block = own_block()
    owners = [pack_ref[0, 0], pack_ref[1, 0], beside_ref[0, 0], beside_ref[1, 0]]
    blocks = [block, block ^ 2, block ^ 1, block ^ 3]
    ids = iota((32, 32), 1)
    place, row = ids // 8, (ids % 8).astype(F32)
    target = jnp.zeros((32, 32), F32)
    for j in range(4):
        own = (blocks[j] * 8).astype(F32) + row
        other = (blocks[j ^ 1] * 8).astype(F32) + owners[j ^ 1]
        target = jnp.where(place == j, jnp.where(row == owners[j], other, own), target)
    order = (target == iota((32, 32), 0).astype(F32)).astype(F32)

    expert = own_expert()
    names_own = jnp.max((turned_ref[...] == expert).astype(F32), axis=0, keepdims=True)
    names_own = jnp.broadcast_to(names_own, (8, 32))
    upper = (iota((32, 32), 0) < iota((32, 32), 1)).astype(F32)
    rank = dot(names_own, upper)
    slots = (iota((8, 32), 0) % 4).astype(F32)
    chooser = jnp.where(names_own > 0, (rank == slots).astype(F32), 0.0)
    gathered = dot(chooser, order)
    member = named_by(turned_ref)
    member_ref[...] = dot(chooser, member)

    tile_row = iota((32, 64), 1) // 16 * 8 + iota((32, 64), 1) % 8
    widen = (tile_row == iota((32, 64), 0)).astype(F32)
    wide = dot(gathered, widen)
    odd = iota((8, 64), 1) // 8 % 2 == 1
    chooser_ref[...] = jnp.concatenate([jnp.where(odd, 0.0, wide), jnp.where(odd, wide, 0.0)], axis=0).astype(BF16)
    first = (iota((8, 32), 1) == iota((8, 32), 0) + block * 8).astype(F32)
    own_wide = dot(dot(first, order), widen)
    tile = lax.axis_index("y") * 4 + lax.axis_index("x")
    own_rows_ref[...] = jnp.where(odd == (tile % 2 == 1), own_wide, 0.0).astype(BF16)
    spread_ref[...] = (iota((128, 1024), 1) // 8 == iota((128, 1024), 0)).astype(BF16)

    lower = (iota((32, 32), 1) < iota((32, 32), 0)).astype(F32)
    slot = jnp.where(member > 0, dot(lower, member), -1.0)
    first = (iota((8, 32), 1) == iota((8, 32), 0) + block * 8).astype(F32)
    slot = dot(first, slot)
    src = iota((128, 256), 1)
    sender = src // 128 * 64 + src % 16 * 4 + src // 16 % 4
    slot = dot(slot, (sender == iota((128, 256), 0)).astype(F32))
    for k in range(4):
        use_ref[k * 8 : (k + 1) * 8, :] = (slot == float(k)).astype(F32)


def fetch_kernel(after_ref, router_hbm, in_hbm, down_hbm, router_ref, in_ref, down_ref, sems):
    pairs = [(router_hbm, router_ref, 1), (in_hbm, in_ref, 8), (down_hbm, down_ref, 4)]
    copies = []
    for source, target, cuts in pairs:
        rows = source.shape[0] // cuts
        for i in range(cuts):
            part = pl.ds(i * rows, rows)
            copies.append(pltpu.make_async_copy(source.at[part], target.at[part], sems.at[len(copies)]))
    for copy in copies:
        copy.start()
    for copy in copies:
        copy.wait()


def sum_kernel(flips, a_ref, b_ref, c_ref, total_ref, out_ref):
    part = dict(zip(flips, (a_ref, b_ref, c_ref)))
    out_ref[...] = (total_ref[...] + part[1][...]) + (part[2][...] + part[3][...])


def hidden_kernel(two_ref, one_ref, three_ref, total_ref, message_ref, got_ref, resid_ref, fresh_ref, out_ref):
    taken = iota((8, 128), 0).astype(F32) == message_ref[4:5, :]
    for pair in range(8):
        parts = []
        for c in (2 * pair, 2 * pair + 1):
            rows = resid_ref[:, c * 128 : (c + 1) * 128].astype(F32)
            total = (total_ref[c] + one_ref[c]) + (two_ref[c] + three_ref[c])
            parts.append(jnp.where(taken, got_ref[8 + c : 9 + c, :], rows) + total)
        out_ref[pair * 16 : (pair + 1) * 16, :] = jnp.concatenate(parts, axis=0).astype(BF16)
    out_ref[128:256, :] = fresh_ref[...]


def expert_kernel(
    own_rows_ref, chooser_ref, member_ref, spread_ref, gain_ref, packet_ref, theirs_ref, next_ref, cross_ref,
    router_ref, in_ref, down_ref, out_ref, own_ref, turn_ref,
):
    expert = own_expert()
    packets = (packet_ref, theirs_ref, next_ref, cross_ref)

    right = beside(*(jnp.concatenate([ref[p * 16 : (p + 1) * 16, :] for ref in packets], axis=0) for p in range(8)))
    both = dot(chooser_ref[...], right)
    tiles = [both[c % 2 * 8 : c % 2 * 8 + 8, c // 2 * 128 : (c // 2 + 1) * 128] for c in range(16)]
    squares = tiles[0] * tiles[0]
    for x in tiles[1:]:
        squares += x * x
    scale = lax.rsqrt(jnp.sum(squares, axis=1, keepdims=True) * (1.0 / 2048) + 1e-06)
    tiles = [x * scale * gain_ref[:, c * 128 : (c + 1) * 128] for c, x in enumerate(tiles)]

    logits = dot(beside(*tiles).astype(BF16), router_ref[...])
    member = member_ref[...]
    chosen = jnp.where(member > 0, 1.0 / (1.0 + jnp.exp(-logits)), 0.0)
    share = jnp.sum(jnp.where(iota((8, 128), 1) == expert, chosen, 0.0), axis=1, keepdims=True)
    share = share / jnp.sum(chosen, axis=1, keepdims=True)
    gates = jnp.where(jnp.sum(member, axis=1, keepdims=True) > 0, share, 0.0)

    stacked = jnp.concatenate(tiles, axis=0)
    repeated = dot(stacked.astype(BF16), spread_ref[...])
    kind = iota((8, 1024), 1) % 8 - iota((8, 1024), 0) // 4
    pre = jnp.zeros((64, 256), F32)
    for c in range(8):
        halves = [repeated[i * 8 : (i + 1) * 8, :] for i in (c, c + 8)]
        left = jnp.concatenate([jnp.where(kind == 2 * p, half, 0.0) for half in halves for p in range(4)], axis=0)
        right = beside(in_ref[c * 1024 : (c + 1) * 1024, :], in_ref[(c + 8) * 1024 : (c + 9) * 1024, :])
        pre += dot(left.astype(BF16), right)
    pre = pre[:32, :128] + pre[32:, 128:]
    acts = []
    for p in range(4):
        both = pre[p * 8 : (p + 1) * 8, :]
        acts.append(both / (1.0 + jnp.exp(-both)) * pltpu.roll(both, 4, 0))
    act = jnp.concatenate(acts, axis=1).astype(BF16)
    for c in range(8):
        part = dot(act, down_ref[:, c * 256 : (c + 1) * 256])
        turn_ref[2 * c] = part[:, :128] * gates
        turn_ref[2 * c + 1] = part[:, 128:] * gates

    lane_block = iota((16, 128), 1) // 32
    by_slot = [turn_ref[:, k, :] for k in range(4)]
    for q in range(4):
        piece = jnp.zeros((16, 128), F32)
        for k in range(4):
            shift = (k - q) * 32 % 128
            moved = by_slot[k] if shift == 0 else pltpu.roll(by_slot[k], shift, 1)
            piece = jnp.where(lane_block == k, moved, piece)
        for b in range(4):
            out_ref[b * 64 + q * 16 : b * 64 + (q + 1) * 16, :] = piece

    tile = lax.axis_index("y") * 4 + lax.axis_index("x")
    rows = pl.ds(pl.multiple_of(tile // 2 * 16, 16), 16)
    mine = dot(own_rows_ref[...], jnp.concatenate([ref[rows, :] for ref in packets], axis=0))
    deep = lax.axis_index("z")
    own = mine
    for q in range(1, 4):
        own = jnp.where(deep == q, pltpu.roll(mine, 128 - q * 32, 1), own)
    own_ref[...] = own


def finish_kernel(use_ref, back_ref, own_ref, out_ref):
    back = back_ref[...]
    high = back.astype(BF16)
    low = (back - high.astype(F32)).astype(BF16)
    use = use_ref[...].astype(BF16)
    total = dot(use, high) + dot(use, low)
    out = own_ref[:, 0:32]
    for k in range(4):
        out += total[k * 8 : (k + 1) * 8, k * 32 : (k + 1) * 32]
    out_ref[...] = out.astype(BF16)


def on_device(
    pre_kv, pre_gate, pre_len, owners, win_len, dec_qkv, dec_gate, state_cache, win_cache,
    head_gain, out_weight, resid, moe_gain, router, routes, w_in, w_down,
):
    qkv = dec_qkv.transpose(1, 0, 2)
    gates = dec_gate.reshape(8)

    message = pl.pallas_call(
        message_kernel,
        out_shape=jax.ShapeDtypeStruct((24, 128), F32),
        in_specs=[ANY] + [HBM] * 3,
        out_specs=VMEM,
        scratch_shapes=[
            pltpu.VMEM((1, 1), jnp.int32),
            pltpu.VMEM((1, 8), F32),
            pltpu.VMEM((3, 8, 128), BF16),
            pltpu.VMEM((8, 2048), BF16),
            pltpu.SemaphoreType.DMA((4,)),
        ],
        compiler_params=params(2),
        name="message",
    )(owners.reshape(1, 1), *stay(gates.reshape(1, 8), qkv, resid))
    got = swap(message, "s", 1)

    own_heads, fresh_state = pl.pallas_call(
        own_rows_kernel,
        out_shape=(jax.ShapeDtypeStruct((8, 128), F32), jax.ShapeDtypeStruct((128, 128), BF16)),
        in_specs=[SMEM] + [HBM] * 8,
        out_specs=(VMEM, VMEM),
        scratch_shapes=[
            pltpu.SMEM((8,), jnp.int32),
            pltpu.SMEM((8,), F32),
            pltpu.VMEM((16, 128), F32),
            pltpu.VMEM((3, 8, 128), BF16),
            pltpu.VMEM((2, 128), F32),
            pltpu.VMEM((2, 2048, 128), BF16),
            pltpu.VMEM((8, 2, 1024, 128), BF16),
            pltpu.VMEM((8, 128, 128), BF16),
            pltpu.SemaphoreType.DMA((5,)),
            pltpu.SemaphoreType.DMA((1,)),
            pltpu.SemaphoreType.DMA((4,)),
            pltpu.SemaphoreType.DMA,
        ],
        compiler_params=params(14),
        name="own_rows",
    )(
        pre_len,
        *stay(
            win_len, gates, pre_gate.reshape(16, 128), qkv, head_gain,
            pre_kv[0], win_cache, state_cache[:, 0],
        )
    )

    partial, pack = pl.pallas_call(
        guest_kernel,
        out_shape=(jax.ShapeDtypeStruct((16, 8, 128), F32), jax.ShapeDtypeStruct((8, 128), F32)),
        in_specs=[SMEM] + [VMEM] * 4 + [HBM] + [VMEM] * 2,
        out_specs=(VMEM, VMEM),
        scratch_shapes=[pltpu.VMEM((2, 128), F32), pltpu.SemaphoreType.DMA],
        compiler_params=params(8),
        name="guest",
    )(pre_len, message, got, own_heads, fresh_state, *stay(head_gain), pre_kv[0], out_weight)

    expert_in = w_in[0].reshape(2048, 2, 4, 128).transpose(0, 2, 1, 3).reshape(16384, 128)
    total = partial
    for axis, flips in (("x", (2, 1, 3)), ("z", (3, 2, 1)), ("y", (2, 1, 3))):
        parts = [swap(total, axis, flip) for flip in flips]
        if axis != "y":
            total = pl.pallas_call(
                functools.partial(sum_kernel, flips),
                out_shape=pltpu.VMEM((16, 8, 128), F32),
                in_specs=[VMEM] * 4,
                out_specs=VMEM,
                compiler_params=params(2),
                name="sum_" + axis,
            )(*parts, total)
    packet = pl.pallas_call(
        hidden_kernel,
        out_shape=jax.ShapeDtypeStruct((256, 128), BF16),
        in_specs=[VMEM] * 8,
        out_specs=VMEM,
        compiler_params=params(2),
        name="hidden",
    )(*parts, total, message, got, resid, fresh_state)
    packet, pack = lax.optimization_barrier((packet, pack))
    theirs = swap(packet, "s", 1)
    next_door = swap(pack, "t", 1)
    router_near, in_near, down_near = pl.pallas_call(
        fetch_kernel,
        out_shape=(
            pltpu.VMEM((2048, 128), BF16),
            pltpu.VMEM((16384, 128), BF16),
            pltpu.VMEM((512, 2048), BF16),
        ),
        in_specs=[ANY] + [HBM] * 3,
        out_specs=(VMEM,) * 3,
        scratch_shapes=[pltpu.SemaphoreType.DMA((13,))],
        compiler_params=params(2),
        name="fetch",
    )(packet, *stay(router, expert_in, w_down[0]))

    beyond = swap(packet, "t", 1)
    own_rows, chooser, member, spread, use = pl.pallas_call(
        prepare_kernel,
        out_shape=(
            jax.ShapeDtypeStruct((8, 64), BF16),
            jax.ShapeDtypeStruct((16, 64), BF16),
            jax.ShapeDtypeStruct((8, 128), F32),
            jax.ShapeDtypeStruct((128, 1024), BF16),
            jax.ShapeDtypeStruct((32, 256), F32),
        ),
        in_specs=[VMEM] * 3,
        out_specs=(VMEM,) * 5,
        compiler_params=params(4),
        name="prepare",
    )(pack, next_door, routes.T)
    theirs, router_near, in_near, down_near, own_rows, chooser, member, spread, use = lax.optimization_barrier(
        (theirs, router_near, in_near, down_near, own_rows, chooser, member, spread, use)
    )
    cross = swap(theirs, "t", 1)
    term, own = pl.pallas_call(
        expert_kernel,
        out_shape=(jax.ShapeDtypeStruct((256, 128), F32), jax.ShapeDtypeStruct((8, 128), F32)),
        in_specs=[VMEM] * 12,
        out_specs=(VMEM, VMEM),
        scratch_shapes=[pltpu.VMEM((16, 8, 128), F32)],
        compiler_params=params(12),
        name="experts",
    )(
        own_rows, chooser, member, spread, moe_gain.reshape(1, 2048), packet, theirs, beyond, cross,
        router_near, in_near, down_near,
    )
    back = lax.all_to_all(term.reshape(256, 1, 128), ("s", "t", "z", "y", "x"), 0, 0, tiled=True)
    layer_out = pl.pallas_call(
        finish_kernel,
        out_shape=jax.ShapeDtypeStruct((8, 32), BF16),
        in_specs=[VMEM] * 3,
        out_specs=VMEM,
        compiler_params=params(2),
        name="finish",
    )(use, back.reshape(256, 128), own)

    late_qkv, late_gate, late_state, late_pack, _ = lax.optimization_barrier(
        (dec_qkv, dec_gate, state_cache, pack, own)
    )
    taken = jnp.arange(8, dtype=F32) == late_pack[0, :8]
    previous = jnp.where(taken[:, None, None], theirs[None, 128:], late_state[:, 0]).astype(F32)
    own_k, own_v = late_qkv[:, 1].astype(F32), late_qkv[:, 2].astype(F32)
    states = jnp.exp(late_gate)[:, :, None] * previous + own_k[:, :, None] * own_v[:, None, :]
    return layer_out, states[:, None]


def solution(mesh):
    fine = Mesh(mesh.devices.reshape(2, 4, 4, 4, 2), ("s", "y", "x", "z", "t"))
    placed = (
        P(BLOCKS, None, None, GRID),
        P(BLOCKS, GRID, None),
        P(BLOCKS),
        P(BLOCKS),
        P(BLOCKS),
        P(BLOCKS, None, GRID),
        P(BLOCKS, GRID),
        P(BLOCKS, GRID, None, None),
        P(BLOCKS, None, None, GRID),
        P(None, GRID),
        P(GRID, None),
        P(BLOCKS, None),
        P(),
        P(),
        P(),
        P(("s",) + GRID, None, None, "t"),
        P(("s",) + GRID, "t", None),
    )
    return jax.shard_map(
        on_device,
        mesh=fine,
        in_specs=placed,
        out_specs=(P(BLOCKS, GRID), P(BLOCKS, GRID, None, None)),
        check_vma=False,
    )
```

```python
import functools

import jax
import jax.numpy as jnp
from jax import lax
from jax.experimental import pallas as pl
from jax.experimental.pallas import tpu as pltpu
from jax.sharding import Mesh, PartitionSpec as P

GRID = ("y", "x", "z")
BLOCKS = ("s", "t")
F32 = jnp.float32
BF16 = jnp.bfloat16
EXACT = lax.Precision.HIGHEST
SCALE = 128 ** (-0.5)

ANY = pl.BlockSpec(memory_space=pl.ANY)
HBM = pl.BlockSpec(memory_space=pl.ANY)
VMEM = pl.BlockSpec(memory_space=pltpu.VMEM)
SMEM = pl.BlockSpec(memory_space=pltpu.SMEM)


def params(mib):
    return pltpu.CompilerParams(vmem_limit_bytes=int(mib * 1024 * 1024))


def stay(*arrays):
    return [pltpu.with_memory_space_constraint(a, pltpu.HBM) for a in arrays]


def swap(shard, axis, flip):
    return lax.ppermute(shard, axis, [(i, i ^ flip) for i in range(lax.axis_size(axis))])


def iota(shape, axis):
    return lax.broadcasted_iota(jnp.int32, shape, axis)


def norm_rows(values, gain_row):
    return values * lax.rsqrt(jnp.mean(values * values, axis=-1, keepdims=True) + 1e-06) * gain_row


def dot(a, b, precision=None):
    return jnp.dot(a, b, preferred_element_type=F32, precision=precision)


def dot_t(a, b):
    return lax.dot_general(a, b, (((1,), (1,)), ((), ())), preferred_element_type=F32)


def beside(*parts):
    return jnp.concatenate(parts, axis=1)


def split_rows(queries):
    odd = iota((8, 128), 0) % 2 == 1
    return beside(jnp.where(odd, 0.0, queries), jnp.where(odd, queries, 0.0)).astype(BF16)


def own_block():
    return lax.axis_index("s") * 2 + lax.axis_index("t")


def picked(rows, index):
    return jnp.sum(jnp.where(iota(rows.shape, 0) == index, rows, 0.0), axis=0, keepdims=True)


def message_kernel(owner_hbm, gate_hbm, qkv_hbm, resid_hbm, out_ref, owner_ref, gate_ref, qkv_ref, resid_ref, sems):
    pairs = [(owner_hbm, owner_ref), (gate_hbm, gate_ref), (qkv_hbm, qkv_ref), (resid_hbm, resid_ref)]
    copies = [pltpu.make_async_copy(a, b, sems.at[i]) for i, (a, b) in enumerate(pairs)]
    for copy in copies:
        copy.start()
    for copy in copies:
        copy.wait()
    owner = owner_ref[...]
    for part in range(3):
        out_ref[part : part + 1, :] = picked(qkv_ref[part].astype(F32), owner)
    gate = jnp.sum(jnp.where(iota((1, 8), 1) == owner, gate_ref[...], 0.0), axis=1, keepdims=True)
    out_ref[3:4, :] = jnp.broadcast_to(gate, (1, 128))
    out_ref[4:8, :] = jnp.broadcast_to(owner.astype(F32), (4, 128))
    row = picked(resid_ref[...].astype(F32), owner)
    for c in range(16):
        out_ref[8 + c : 9 + c, :] = row[:, c * 128 : (c + 1) * 128]


def own_rows_kernel(
    length_ref, live_hbm, gate_hbm, decay_hbm, qkv_hbm, gain_hbm, kv_hbm, cache_hbm, state_hbm,
    head_ref, fresh_ref, live_ref, gate_ref, decay_ref, qkv_ref, gain_ref, kv_ref, cache_ref, state_ref,
    small_sem, kv_sem, cache_sem, state_sem,
):
    small = [
        (decay_hbm, decay_ref), (qkv_hbm, qkv_ref), (live_hbm, live_ref),
        (gate_hbm, gate_ref), (gain_hbm, gain_ref),
    ]
    small_copies = [pltpu.make_async_copy(a, b, small_sem.at[i]) for i, (a, b) in enumerate(small)]
    kv_copies = [pltpu.make_async_copy(kv_hbm, kv_ref, kv_sem.at[0])]
    state_copy = pltpu.make_async_copy(state_hbm, state_ref, state_sem)
    cache_copies = [
        pltpu.make_async_copy(cache_hbm.at[pl.ds(2 * p, 2)], cache_ref.at[pl.ds(2 * p, 2)], cache_sem.at[p]) for p in range(4)
    ]
    for copy in small_copies + kv_copies + cache_copies + [state_copy]:
        copy.start()

    for copy in small_copies:
        copy.wait()
    length = length_ref[0]
    places = iota((16, 128), 0) * 128 + iota((16, 128), 1)
    kept = jnp.where(places < length, decay_ref[...], 0.0)
    later = (iota((128, 128), 0) > iota((128, 128), 1)).astype(F32)
    later_rows = (iota((16, 16), 1) > iota((16, 16), 0)).astype(F32)
    totals = jnp.broadcast_to(jnp.sum(kept, axis=1, keepdims=True), (16, 128))
    suffix = dot(kept, later, EXACT) + dot(later_rows, totals, EXACT)
    weights = jnp.where(places < length, jnp.exp(suffix), 0.0)

    for copy in kv_copies:
        copy.wait()
    fresh = jnp.zeros((128, 128), F32)
    for i in range(8):
        parts = []
        for j in (2 * i, 2 * i + 1):
            turned = kv_ref[0, j * 128 : (j + 1) * 128, :].T.astype(F32)
            parts.append((turned * weights[j : j + 1, :]).astype(BF16))
        fresh += dot(beside(*parts), kv_ref[1, i * 256 : (i + 1) * 256, :])
    fresh_ref[...] = fresh.astype(BF16)

    queries = qkv_ref[0]
    q32, k32, v32 = queries.astype(F32), qkv_ref[1].astype(F32), qkv_ref[2].astype(F32)
    self_raw = jnp.sum(q32 * k32, axis=1, keepdims=True)
    self_score = self_raw * SCALE
    scores = jnp.zeros((8, 1024), F32)
    live = jnp.zeros((8, 1024), jnp.int32)
    gate = jnp.zeros((8, 128), F32)
    halves = split_rows(q32)
    for r in range(8):
        live = jnp.where(iota((8, 1024), 0) == r, live_ref[r], live)
        gate = jnp.where(iota((8, 128), 0) == r, gate_ref[r], gate)
    for p in range(4):
        cache_copies[p].wait()
        both = dot_t(halves, beside(cache_ref[2 * p, 0], cache_ref[2 * p + 1, 0]))
        scores = jnp.where(iota((8, 1024), 0) // 2 == p, both, scores)
    scores = scores * SCALE
    alive = iota((8, 1024), 1) >= 1024 - live
    peak = jnp.max(jnp.where(alive, scores, -jnp.inf), axis=1, keepdims=True)
    peak = jnp.maximum(peak, self_score)
    prob = jnp.where(alive, jnp.exp(scores - peak), 0.0).astype(BF16)
    self_prob = jnp.exp(self_score - peak).astype(BF16).astype(F32)
    below = jnp.sum(prob.astype(F32), axis=1, keepdims=True) + self_prob
    above = jnp.zeros((8, 128), F32)
    linear = jnp.zeros((8, 128), F32)
    state_copy.wait()
    row = iota((8, 128), 0)
    for p in range(4):
        both = dot(prob, beside(cache_ref[2 * p, 1], cache_ref[2 * p + 1, 1]))
        above = jnp.where(row == 2 * p, both[:, :128], jnp.where(row == 2 * p + 1, both[:, 128:], above))
    for p in range(2):
        a, b, c, d = (state_ref[4 * p + i] for i in range(4))
        both = dot(halves, jnp.concatenate([beside(a, c), beside(b, d)], axis=0))
        linear = jnp.where(row // 2 == 2 * p, both[:, :128], jnp.where(row // 2 == 2 * p + 1, both[:, 128:], linear))
    window_out = (above + self_prob * v32) / below
    linear_out = jnp.exp(gate) * linear + self_raw * v32
    head_ref[...] = norm_rows(linear_out, gain_ref[0:1, :]) + norm_rows(window_out, gain_ref[1:2, :])


def guest_kernel(
    length_ref, message_ref, got_ref, head_ref, fresh_ref, gain_hbm, kv_ref, weight_ref,
    out_ref, pack_ref, gain_ref, gain_sem,
):
    gain_copy = pltpu.make_async_copy(gain_hbm, gain_ref, gain_sem)
    gain_copy.start()
    owner = message_ref[4:5, :]
    rows = iota((8, 128), 0).astype(F32)
    pack_ref[...] = jnp.where(rows == 0.0, owner, got_ref[4:5, :])
    q32, k32, v32 = got_ref[0:1, :], got_ref[1:2, :], got_ref[2:3, :]
    self_raw = jnp.sum(q32 * k32, axis=1, keepdims=True)
    self_score = self_raw * SCALE
    query = jnp.broadcast_to(q32, (8, 128))
    linear_out = jnp.exp(got_ref[3:4, :]) * dot(query.astype(BF16), fresh_ref[...])[0:1, :] + self_raw * v32

    scores = dot_t(split_rows(query), beside(kv_ref[0, 0:1024, :], kv_ref[0, 1024:2048, :])) * SCALE
    places = iota((8, 1024), 1) + iota((8, 1024), 0) % 2 * 1024
    length = length_ref[0]
    alive = (places < length) & (places >= length - 1024)
    peak = jnp.max(jnp.where(alive, scores, -jnp.inf), axis=1, keepdims=True)
    peak = jnp.maximum(jnp.maximum(peak[0:1, :], peak[1:2, :]), self_score)
    prob = jnp.where(alive, jnp.exp(scores - peak), 0.0).astype(BF16)
    self_prob = jnp.exp(self_score - peak).astype(BF16).astype(F32)
    total = jnp.sum(prob.astype(F32), axis=1, keepdims=True)
    below = total[0:1, :] + total[1:2, :] + self_prob
    both = dot(prob, beside(kv_ref[1, 0:1024, :], kv_ref[1, 1024:2048, :]))
    window_out = (both[0:1, :128] + both[1:2, 128:] + self_prob * v32) / below
    gain_copy.wait()
    head = norm_rows(linear_out, gain_ref[0:1, :]) + norm_rows(window_out, gain_ref[1:2, :])
    head = jnp.where(rows == owner, head, head_ref[...]).astype(BF16)
    for c in range(8):
        part = dot(head, weight_ref[:, c * 256 : (c + 1) * 256])
        out_ref[2 * c] = part[:, :128]
        out_ref[2 * c + 1] = part[:, 128:]


def named_by(turned_ref):
    turned = turned_ref[...]
    experts = iota((128, 32), 0)
    member = jnp.zeros((128, 32), F32)
    for k in range(8):
        member = jnp.where(turned[k : k + 1, :] == experts, 1.0, member)
    same = (iota((32, 32), 0) == iota((32, 32), 1)).astype(F32)
    return dot_t(same, member)


def own_expert():
    return lax.axis_index("s") * 64 + lax.axis_index("y") * 16 + lax.axis_index("x") * 4 + lax.axis_index("z")


def prepare_kernel(
    pack_ref, beside_ref, turned_ref, own_rows_ref, chooser_ref, member_ref, spread_ref, use_ref
):
    block = own_block()
    owners = [pack_ref[0, 0], pack_ref[1, 0], beside_ref[0, 0], beside_ref[1, 0]]
    blocks = [block, block ^ 2, block ^ 1, block ^ 3]
    ids = iota((32, 32), 1)
    place, row = ids // 8, (ids % 8).astype(F32)
    target = jnp.zeros((32, 32), F32)
    for j in range(4):
        own = (blocks[j] * 8).astype(F32) + row
        other = (blocks[j ^ 1] * 8).astype(F32) + owners[j ^ 1]
        target = jnp.where(place == j, jnp.where(row == owners[j], other, own), target)
    order = (target == iota((32, 32), 0).astype(F32)).astype(F32)

    expert = own_expert()
    names_own = jnp.max((turned_ref[...] == expert).astype(F32), axis=0, keepdims=True)
    names_own = jnp.broadcast_to(names_own, (8, 32))
    upper = (iota((32, 32), 0) < iota((32, 32), 1)).astype(F32)
    rank = dot(names_own, upper)
    slots = (iota((8, 32), 0) % 4).astype(F32)
    chooser = jnp.where(names_own > 0, (rank == slots).astype(F32), 0.0)
    gathered = dot(chooser, order)
    member = named_by(turned_ref)
    member_ref[...] = dot(chooser, member)

    tile_row = iota((32, 64), 1) // 16 * 8 + iota((32, 64), 1) % 8
    widen = (tile_row == iota((32, 64), 0)).astype(F32)
    wide = dot(gathered, widen)
    odd = iota((8, 64), 1) // 8 % 2 == 1
    chooser_ref[...] = jnp.concatenate([jnp.where(odd, 0.0, wide), jnp.where(odd, wide, 0.0)], axis=0).astype(BF16)
    first = (iota((8, 32), 1) == iota((8, 32), 0) + block * 8).astype(F32)
    own_wide = dot(dot(first, order), widen)
    tile = lax.axis_index("y") * 4 + lax.axis_index("x")
    own_rows_ref[...] = jnp.where(odd == (tile % 2 == 1), own_wide, 0.0).astype(BF16)
    spread_ref[...] = (iota((128, 1024), 1) // 8 == iota((128, 1024), 0)).astype(BF16)

    lower = (iota((32, 32), 1) < iota((32, 32), 0)).astype(F32)
    slot = jnp.where(member > 0, dot(lower, member), -1.0)
    first = (iota((8, 32), 1) == iota((8, 32), 0) + block * 8).astype(F32)
    slot = dot(first, slot)
    src = iota((128, 256), 1)
    sender = src // 128 * 64 + src % 16 * 4 + src // 16 % 4
    slot = dot(slot, (sender == iota((128, 256), 0)).astype(F32))
    for k in range(4):
        use_ref[k * 8 : (k + 1) * 8, :] = (slot == float(k)).astype(F32)


def fetch_kernel(after_ref, router_hbm, in_hbm, down_hbm, router_ref, in_ref, down_ref, sems):
    pairs = [(router_hbm, router_ref, 1), (in_hbm, in_ref, 8), (down_hbm, down_ref, 4)]
    copies = []
    for source, target, cuts in pairs:
        rows = source.shape[0] // cuts
        for i in range(cuts):
            part = pl.ds(i * rows, rows)
            copies.append(pltpu.make_async_copy(source.at[part], target.at[part], sems.at[len(copies)]))
    for copy in copies:
        copy.start()
    for copy in copies:
        copy.wait()


def sum_kernel(flips, a_ref, b_ref, c_ref, total_ref, out_ref):
    part = dict(zip(flips, (a_ref, b_ref, c_ref)))
    out_ref[...] = (total_ref[...] + part[1][...]) + (part[2][...] + part[3][...])


def hidden_kernel(two_ref, one_ref, three_ref, total_ref, message_ref, got_ref, resid_ref, fresh_ref, out_ref):
    taken = iota((8, 128), 0).astype(F32) == message_ref[4:5, :]
    for pair in range(8):
        parts = []
        for c in (2 * pair, 2 * pair + 1):
            rows = resid_ref[:, c * 128 : (c + 1) * 128].astype(F32)
            total = (total_ref[c] + one_ref[c]) + (two_ref[c] + three_ref[c])
            parts.append(jnp.where(taken, got_ref[8 + c : 9 + c, :], rows) + total)
        out_ref[pair * 16 : (pair + 1) * 16, :] = jnp.concatenate(parts, axis=0).astype(BF16)
    out_ref[128:256, :] = fresh_ref[...]


def expert_kernel(
    own_rows_ref, chooser_ref, member_ref, spread_ref, gain_ref, packet_ref, theirs_ref, next_ref, cross_ref,
    router_ref, in_ref, down_ref, out_ref, own_ref, turn_ref,
):
    expert = own_expert()
    packets = (packet_ref, theirs_ref, next_ref, cross_ref)

    right = beside(*(jnp.concatenate([ref[p * 16 : (p + 1) * 16, :] for ref in packets], axis=0) for p in range(8)))
    both = dot(chooser_ref[...], right)
    tiles = [both[c % 2 * 8 : c % 2 * 8 + 8, c // 2 * 128 : (c // 2 + 1) * 128] for c in range(16)]
    squares = tiles[0] * tiles[0]
    for x in tiles[1:]:
        squares += x * x
    scale = lax.rsqrt(jnp.sum(squares, axis=1, keepdims=True) * (1.0 / 2048) + 1e-06)
    tiles = [x * scale * gain_ref[:, c * 128 : (c + 1) * 128] for c, x in enumerate(tiles)]

    logits = dot(beside(*tiles).astype(BF16), router_ref[...])
    member = member_ref[...]
    chosen = jnp.where(member > 0, 1.0 / (1.0 + jnp.exp(-logits)), 0.0)
    share = jnp.sum(jnp.where(iota((8, 128), 1) == expert, chosen, 0.0), axis=1, keepdims=True)
    share = share / jnp.sum(chosen, axis=1, keepdims=True)
    gates = jnp.where(jnp.sum(member, axis=1, keepdims=True) > 0, share, 0.0)

    stacked = jnp.concatenate(tiles, axis=0)
    repeated = dot(stacked.astype(BF16), spread_ref[...])
    kind = iota((8, 1024), 1) % 8 - iota((8, 1024), 0) // 4
    pre = jnp.zeros((64, 256), F32)
    for c in range(8):
        halves = [repeated[i * 8 : (i + 1) * 8, :] for i in (c, c + 8)]
        left = jnp.concatenate([jnp.where(kind == 2 * p, half, 0.0) for half in halves for p in range(4)], axis=0)
        right = beside(in_ref[c * 1024 : (c + 1) * 1024, :], in_ref[(c + 8) * 1024 : (c + 9) * 1024, :])
        pre += dot(left.astype(BF16), right)
    pre = pre[:32, :128] + pre[32:, 128:]
    acts = []
    for p in range(4):
        both = pre[p * 8 : (p + 1) * 8, :]
        acts.append(both / (1.0 + jnp.exp(-both)) * pltpu.roll(both, 4, 0))
    act = jnp.concatenate(acts, axis=1).astype(BF16)
    for c in range(8):
        part = dot(act, down_ref[:, c * 256 : (c + 1) * 256])
        turn_ref[2 * c] = part[:, :128] * gates
        turn_ref[2 * c + 1] = part[:, 128:] * gates

    lane_block = iota((16, 128), 1) // 32
    by_slot = [turn_ref[:, k, :] for k in range(4)]
    for q in range(4):
        piece = jnp.zeros((16, 128), F32)
        for k in range(4):
            shift = (k - q) * 32 % 128
            moved = by_slot[k] if shift == 0 else pltpu.roll(by_slot[k], shift, 1)
            piece = jnp.where(lane_block == k, moved, piece)
        for b in range(4):
            out_ref[b * 64 + q * 16 : b * 64 + (q + 1) * 16, :] = piece

    tile = lax.axis_index("y") * 4 + lax.axis_index("x")
    rows = pl.ds(pl.multiple_of(tile // 2 * 16, 16), 16)
    mine = dot(own_rows_ref[...], jnp.concatenate([ref[rows, :] for ref in packets], axis=0))
    deep = lax.axis_index("z")
    own = mine
    for q in range(1, 4):
        own = jnp.where(deep == q, pltpu.roll(mine, 128 - q * 32, 1), own)
    own_ref[...] = own


def finish_kernel(use_ref, back_ref, own_ref, out_ref):
    back = back_ref[...]
    high = back.astype(BF16)
    low = (back - high.astype(F32)).astype(BF16)
    use = use_ref[...].astype(BF16)
    total = dot(use, high) + dot(use, low)
    out = own_ref[:, 0:32]
    for k in range(4):
        out += total[k * 8 : (k + 1) * 8, k * 32 : (k + 1) * 32]
    out_ref[...] = out.astype(BF16)


def on_device(
    pre_kv, pre_gate, pre_len, owners, win_len, dec_qkv, dec_gate, state_cache, win_cache,
    head_gain, out_weight, resid, moe_gain, router, routes, w_in, w_down,
):
    qkv = dec_qkv.transpose(1, 0, 2)
    gates = dec_gate.reshape(8)

    message = pl.pallas_call(
        message_kernel,
        out_shape=jax.ShapeDtypeStruct((24, 128), F32),
        in_specs=[ANY] + [HBM] * 3,
        out_specs=VMEM,
        scratch_shapes=[
            pltpu.VMEM((1, 1), jnp.int32),
            pltpu.VMEM((1, 8), F32),
            pltpu.VMEM((3, 8, 128), BF16),
            pltpu.VMEM((8, 2048), BF16),
            pltpu.SemaphoreType.DMA((4,)),
        ],
        compiler_params=params(2),
        name="message",
    )(owners.reshape(1, 1), *stay(gates.reshape(1, 8), qkv, resid))
    got = swap(message, "s", 1)

    own_heads, fresh_state = pl.pallas_call(
        own_rows_kernel,
        out_shape=(jax.ShapeDtypeStruct((8, 128), F32), jax.ShapeDtypeStruct((128, 128), BF16)),
        in_specs=[SMEM] + [HBM] * 8,
        out_specs=(VMEM, VMEM),
        scratch_shapes=[
            pltpu.SMEM((8,), jnp.int32),
            pltpu.SMEM((8,), F32),
            pltpu.VMEM((16, 128), F32),
            pltpu.VMEM((3, 8, 128), BF16),
            pltpu.VMEM((2, 128), F32),
            pltpu.VMEM((2, 2048, 128), BF16),
            pltpu.VMEM((8, 2, 1024, 128), BF16),
            pltpu.VMEM((8, 128, 128), BF16),
            pltpu.SemaphoreType.DMA((5,)),
            pltpu.SemaphoreType.DMA((1,)),
            pltpu.SemaphoreType.DMA((4,)),
            pltpu.SemaphoreType.DMA,
        ],
        compiler_params=params(14),
        name="own_rows",
    )(
        pre_len,
        *stay(
            win_len, gates, pre_gate.reshape(16, 128), qkv, head_gain,
            pre_kv[0], win_cache, state_cache[:, 0],
        )
    )

    partial, pack = pl.pallas_call(
        guest_kernel,
        out_shape=(jax.ShapeDtypeStruct((16, 8, 128), F32), jax.ShapeDtypeStruct((8, 128), F32)),
        in_specs=[SMEM] + [VMEM] * 4 + [HBM] + [VMEM] * 2,
        out_specs=(VMEM, VMEM),
        scratch_shapes=[pltpu.VMEM((2, 128), F32), pltpu.SemaphoreType.DMA],
        compiler_params=params(8),
        name="guest",
    )(pre_len, message, got, own_heads, fresh_state, *stay(head_gain), pre_kv[0], out_weight)

    expert_in = w_in[0].reshape(2048, 2, 4, 128).transpose(0, 2, 1, 3).reshape(16384, 128)
    total = partial
    for axis, flips in (("y", (2, 1, 3)), ("z", (3, 2, 1)), ("x", (2, 1, 3))):
        parts = [swap(total, axis, flip) for flip in flips]
        if axis != "x":
            total = pl.pallas_call(
                functools.partial(sum_kernel, flips),
                out_shape=pltpu.VMEM((16, 8, 128), F32),
                in_specs=[VMEM] * 4,
                out_specs=VMEM,
                compiler_params=params(2),
                name="sum_" + axis,
            )(*parts, total)
    packet = pl.pallas_call(
        hidden_kernel,
        out_shape=jax.ShapeDtypeStruct((256, 128), BF16),
        in_specs=[VMEM] * 8,
        out_specs=VMEM,
        compiler_params=params(2),
        name="hidden",
    )(*parts, total, message, got, resid, fresh_state)
    packet, pack = lax.optimization_barrier((packet, pack))
    theirs = swap(packet, "s", 1)
    next_door = swap(pack, "t", 1)
    router_near, in_near, down_near = pl.pallas_call(
        fetch_kernel,
        out_shape=(
            pltpu.VMEM((2048, 128), BF16),
            pltpu.VMEM((16384, 128), BF16),
            pltpu.VMEM((512, 2048), BF16),
        ),
        in_specs=[ANY] + [HBM] * 3,
        out_specs=(VMEM,) * 3,
        scratch_shapes=[pltpu.SemaphoreType.DMA((13,))],
        compiler_params=params(2),
        name="fetch",
    )(packet, *stay(router, expert_in, w_down[0]))

    beyond = swap(packet, "t", 1)
    own_rows, chooser, member, spread, use = pl.pallas_call(
        prepare_kernel,
        out_shape=(
            jax.ShapeDtypeStruct((8, 64), BF16),
            jax.ShapeDtypeStruct((16, 64), BF16),
            jax.ShapeDtypeStruct((8, 128), F32),
            jax.ShapeDtypeStruct((128, 1024), BF16),
            jax.ShapeDtypeStruct((32, 256), F32),
        ),
        in_specs=[VMEM] * 3,
        out_specs=(VMEM,) * 5,
        compiler_params=params(4),
        name="prepare",
    )(pack, next_door, routes.T)
    theirs, router_near, in_near, down_near, own_rows, chooser, member, spread, use = lax.optimization_barrier(
        (theirs, router_near, in_near, down_near, own_rows, chooser, member, spread, use)
    )
    cross = swap(theirs, "t", 1)
    term, own = pl.pallas_call(
        expert_kernel,
        out_shape=(jax.ShapeDtypeStruct((256, 128), F32), jax.ShapeDtypeStruct((8, 128), F32)),
        in_specs=[VMEM] * 12,
        out_specs=(VMEM, VMEM),
        scratch_shapes=[pltpu.VMEM((16, 8, 128), F32)],
        compiler_params=params(12),
        name="experts",
    )(
        own_rows, chooser, member, spread, moe_gain.reshape(1, 2048), packet, theirs, beyond, cross,
        router_near, in_near, down_near,
    )
    back = lax.all_to_all(term.reshape(256, 1, 128), ("s", "t", "z", "y", "x"), 0, 0, tiled=True)
    layer_out = pl.pallas_call(
        finish_kernel,
        out_shape=jax.ShapeDtypeStruct((8, 32), BF16),
        in_specs=[VMEM] * 3,
        out_specs=VMEM,
        compiler_params=params(2),
        name="finish",
    )(use, back.reshape(256, 128), own)

    late_qkv, late_gate, late_state, late_pack, _ = lax.optimization_barrier(
        (dec_qkv, dec_gate, state_cache, pack, own)
    )
    taken = jnp.arange(8, dtype=F32) == late_pack[0, :8]
    previous = jnp.where(taken[:, None, None], theirs[None, 128:], late_state[:, 0]).astype(F32)
    own_k, own_v = late_qkv[:, 1].astype(F32), late_qkv[:, 2].astype(F32)
    states = jnp.exp(late_gate)[:, :, None] * previous + own_k[:, :, None] * own_v[:, None, :]
    return layer_out, states[:, None]


def solution(mesh):
    fine = Mesh(mesh.devices.reshape(2, 4, 4, 4, 2), ("s", "y", "x", "z", "t"))
    placed = (
        P(BLOCKS, None, None, GRID),
        P(BLOCKS, GRID, None),
        P(BLOCKS),
        P(BLOCKS),
        P(BLOCKS),
        P(BLOCKS, None, GRID),
        P(BLOCKS, GRID),
        P(BLOCKS, GRID, None, None),
        P(BLOCKS, None, None, GRID),
        P(None, GRID),
        P(GRID, None),
        P(BLOCKS, None),
        P(),
        P(),
        P(),
        P(("s",) + GRID, None, None, "t"),
        P(("s",) + GRID, "t", None),
    )
    return jax.shard_map(
        on_device,
        mesh=fine,
        in_specs=placed,
        out_specs=(P(BLOCKS, GRID), P(BLOCKS, GRID, None, None)),
        check_vma=False,
    )
```
